32 devices in a mesh: gx: 4 (over y, x), gy: 8 (over z, core).
Axes of the slice: x: 2, y: 2, z: 4, core: 2. Of those that a mesh axis runs over, the one named last changes fastest.
Arguments:
- velocity: float32 [3, 2, 512, 1024], P(None, None, 'gx', 'gy'), may hold values from -8 to 8
- diffusion: float32 [2, 512, 1024], P(None, 'gx', 'gy'), may hold values from 16384 to 262144
Outputs:
- new_velocity: float32 [3, 2, 512, 1024], P(None, None, 'gx', 'gy')
The draws below stay inside these ranges and needn't reach their ends.
All inputs are finite; a program needn't handle non-finite values.
Results may differ from the reference program's by a relative error of at most 0.000024.
Values sent between devices are 32-bit elements; how exact they have to be, the bound alone decides.
A program may use at most 64 MiB of HBM per device.

```python
import math
import jax
import jax.numpy as jnp
from jax import lax

PLANES = 2
NX = 512
NY = 1024


def draw_velocity(key, part):
    keys = jax.random.split(jax.random.fold_in(key, 17), 4)
    waves_x = jax.random.randint(keys[0], (3, PLANES, 8), 1, 7).astype(jnp.float32)
    waves_y = jax.random.randint(keys[1], (3, PLANES, 8), 1, 7).astype(jnp.float32)
    phases = jax.random.uniform(keys[2], (2, 3, PLANES, 8), jnp.float32, 0.0, 6.2831853)
    coord_x = jnp.arange(NX, dtype=jnp.float32) / NX
    coord_y = jnp.arange(NY, dtype=jnp.float32) / NY
    along_x = jnp.cos(6.2831853 * waves_x[..., None] * coord_x + phases[0][..., None])
    along_y = jnp.cos(6.2831853 * waves_y[..., None] * coord_y + phases[1][..., None])
    smooth = 0.35 * jnp.einsum('cpkx,cpky->cpxy', along_x, along_y)
    rough = jnp.clip(0.5 * jax.random.normal(keys[3], (3, PLANES, NX, NY), jnp.float32), -3.0, 3.0)
    stream = 1.0
    mean_flow = jnp.array([stream, 0.0, 0.0], jnp.float32)[:, None, None, None]
    return (smooth + rough + mean_flow).astype(jnp.float32)


def level_of(key, shape, cuts, low, largest):
    gain, own = 1.0, jax.random.fold_in(key, 6)
    for position, shards_of in cuts:
        steps = jnp.exp(jax.random.uniform(jax.random.fold_in(own, position), (shards_of,), jnp.float32, low / len(cuts), largest / len(cuts)))
        gain = gain * jnp.repeat(steps, shape[position] // shards_of).reshape([-1 if axis == position else 1 for axis in range(len(shape))])
    return gain


def setup_inputs(seed: int = 0) -> dict:
    key_list = jax.random.split(jax.random.key(seed), 3)
    return {
        "velocity": draw_velocity(jax.random.fold_in(key_list[2], 71), 0),
        "diffusion": jnp.clip(jnp.exp(math.log(262144.0) - 2.7725887 * jax.random.uniform(key_list[1], (PLANES, NX, NY), jnp.float32) ** level_of(key_list[1], (PLANES, NX, NY), ((1, 4), (2, 8)), -0.2, 0.2)), 16384.0, 262144.0),
    }


courant = 0.25


def thomas(source, lower_face, upper_face, cell_dim):
    source_t = jnp.moveaxis(source, cell_dim, 0)
    lower_t = jnp.moveaxis(lower_face, cell_dim - 1, 0)
    upper_t = jnp.moveaxis(upper_face, cell_dim - 1, 0)

    def downward(state, entries):
        share_prev, value_prev = state
        low_now, high_now, src_now = entries
        denom = 1.0 + high_now + low_now * share_prev
        share_next = (1.0 + low_now * share_prev) / denom
        value_next = (src_now + low_now * value_prev) / denom
        return (share_next, value_next), (share_next, value_next)

    start = (jnp.ones(lower_t.shape[1:], jnp.float32), jnp.zeros(source_t.shape[1:], jnp.float32))
    unused, (share_all, value_all) = lax.scan(downward, start, (lower_t, upper_t, source_t))

    def upward(w_next, entries):
        share_now, value_now = entries
        w_now = value_now + (1.0 - share_now) * w_next
        return w_now, w_now

    unused_two, w_all = lax.scan(upward, jnp.zeros(source_t.shape[1:], jnp.float32), (share_all, value_all), reverse=True)
    return jnp.moveaxis(w_all, 0, cell_dim)


def reference(velocity, diffusion):
    padded = jnp.pad(velocity, ((0, 0), (0, 0), (1, 1), (1, 1)))
    grad_x = padded[:, :, 2:, 1:-1] - padded[:, :, :-2, 1:-1]
    grad_y = padded[:, :, 1:-1, 2:] - padded[:, :, 1:-1, :-2]
    source = velocity - (0.5 * courant) * (velocity[0] * grad_x + velocity[1] * grad_y)
    viscous = jnp.pad(diffusion, ((0, 0), (1, 1), (1, 1)))
    lower_x = 0.5 * (viscous[:, :-2, 1:-1] + diffusion)
    upper_x = 0.5 * (viscous[:, 2:, 1:-1] + diffusion)
    lower_y = 0.5 * (viscous[:, 1:-1, :-2] + diffusion)
    upper_y = 0.5 * (viscous[:, 1:-1, 2:] + diffusion)
    middle = thomas(source, lower_x, upper_x, 2)
    return thomas(middle, lower_y, upper_y, 3)
```

```python
import functools

import jax
import jax.numpy as jnp
from jax import lax
from jax.experimental import pallas as pl
from jax.experimental.pallas import tpu as pltpu
from jax.sharding import PartitionSpec as P

courant = 0.25
SUB = 8
MESH = pl.DeviceIdType.MESH


def halves(a):
    a = a.reshape((a.shape[0] // 2, 2) + a.shape[1:])
    return a[:, 0], a[:, 1]


def plus(a, b):
    return b if a is None else (a if b is None else a + b)


def join_matrix(c1, c2, gr1, gl2, gl1, gr2):
    g = plus(gr1, gl2)
    r = 1.0 / (c1 + c2 + g)
    p, q = c1 * r, c2 * r
    return (p, q, r), p * c2, plus(gl1, p * g), gr2 + q * g


def tree_matrix(c, gl, gr):
    levels = []
    while c.shape[0] > 1:
        c1, c2 = halves(c)
        gr1, gr2 = halves(gr)
        gl1, gl2 = (None, None) if gl is None else halves(gl)
        level, c, gl, gr = join_matrix(c1, c2, gr1, gl2, gl1, gr2)
        levels.append(level)
    return levels, c[0], gl[0], gr[0]


def tree_source(il, ir, levels, widen):
    mids = []
    for level in levels:
        p, q, r = (widen(a) for a in level)
        ir1, ir2 = halves(ir)
        il1, il2 = (None, None) if il is None else halves(il)
        i = plus(ir1, il2)
        mids.append(i * r)
        il = plus(il1, p * i)
        ir = ir2 + q * i
    return mids, il[0], ir[0]


def tree_down(left, right, levels, mids, widen):
    w = right[None]
    for level, mid in zip(reversed(levels), reversed(mids)):
        p, q = widen(level[0]), widen(level[1])
        wl = left[None] if w.shape[0] == 1 else jnp.concatenate([left[None], w[:-1]], 0)
        m = mid + p * wl + q * w
        w = jnp.stack([m, w], 1).reshape((2 * w.shape[0],) + w.shape[1:])
    return w


def roll_rows(a, shift):
    flat = a.reshape((-1,) + a.shape[-2:])
    out = [pltpu.roll(flat[k], shift % SUB, 0) for k in range(flat.shape[0])]
    return jnp.stack(out).reshape(a.shape)


def rows_matrix(c, gl, gr):
    levels = []
    for shift in (1, 2, 4):
        level, c, gl, gr = join_matrix(
            roll_rows(c, shift), c, roll_rows(gr, shift), gl, roll_rows(gl, shift), gr
        )
        levels.append(level)
    return levels, c, gl, gr


def rows_source(il, ir, levels):
    mids = []
    for shift, (p, q, r) in zip((1, 2, 4), levels):
        i = roll_rows(ir, shift) + il
        mids.append(i * r)
        il = roll_rows(il, shift) + p * i
        ir = ir + q * i
    return mids, il, ir


def rows_down(left, right, levels, mids, row):
    def solve(k, wl, wr):
        return mids[k] + levels[k][0] * wl + levels[k][1] * wr

    m = solve(2, left, right)
    m3 = jnp.broadcast_to(m[..., 7:8, :], m.shape)
    wr = jnp.where(row < 4, m3, right)
    m = solve(1, jnp.where(row < 4, left, m3), wr)
    m1 = jnp.broadcast_to(m[..., 3:4, :], m.shape)
    m5 = jnp.broadcast_to(m[..., 7:8, :], m.shape)
    wl = jnp.where(row < 2, left, jnp.where(row < 4, m1, jnp.where(row < 6, m3, m5)))
    wr = jnp.where(row < 2, m1, jnp.where(row < 4, m3, jnp.where(row < 6, m5, right)))
    m = solve(0, wl, wr)
    w = jnp.where(row % 2 == 1, wr, roll_rows(m, 7))
    return jnp.where(row == 0, left, roll_rows(w, 1)), w


def spread(tile, first):
    row = lax.broadcasted_iota(jnp.int32, tile.shape, 1)
    return jnp.where(row % 2 == 0, tile[:, first : first + 1], tile[:, first + 1 : first + 2])


def kernel(
    dx, dy, vel, dif, out,
    xh_send, xh_recv, yh_send, yh_recv, xg, ym, yr, wx, wy, scr, scr_d,
    hs, hr, xs, xr, yms, ymr, yrs, yrr,
):
    ncomp, planes, nx, ny = vel.shape
    tx, ty = nx // SUB, ny // SUB
    nf = ncomp * planes
    ix, iy = lax.axis_index("gx"), lax.axis_index("gy")
    x_peers = [lax.rem(ix + o, dx) for o in range(1, dx)]
    y_peers = [lax.rem(iy + o, dy) for o in range(1, dy)]

    barrier = pltpu.get_barrier_semaphore()
    for peer in x_peers:
        pl.semaphore_signal(barrier, inc=1, device_id={"gx": peer}, device_id_type=MESH)
    for peer in y_peers:
        pl.semaphore_signal(barrier, inc=1, device_id={"gy": peer}, device_id_type=MESH)

    def copy(src, dst, send, recv, where):
        return pltpu.make_async_remote_copy(
            src_ref=src, dst_ref=dst, send_sem=send, recv_sem=recv,
            device_id=where, device_id_type=MESH,
        )

    def wide(a):
        return a[:, None]

    row = lax.broadcasted_iota(jnp.int32, (SUB, ny), 0)
    row_y = lax.broadcasted_iota(jnp.int32, (SUB, nx), 0)
    lane = lax.broadcasted_iota(jnp.int32, (nx, ny), 1)

    v = jnp.stack([vel[:, :, pl.ds(t, SUB, stride=tx), :] for t in range(tx)])
    d = jnp.stack([dif[:, pl.ds(t, SUB, stride=tx), :] for t in range(tx)])
    fields = [v[:, c, p].reshape(nx, ny) for c in range(ncomp) for p in range(planes)]
    fields += [d[:, p].reshape(nx, ny) for p in range(planes)]

    for f in range(nf + planes):
        ref = vel.at[f // planes, f % planes] if f < nf else dif.at[f - nf]
        xh_send[0, f : f + 1, :] = ref[nx - 1 : nx, :]
        xh_send[1, f : f + 1, :] = ref[0:1, :]
    edges = jnp.zeros((nx, ny), jnp.float32)
    for f, a in enumerate(fields):
        edges = jnp.where(lane // 2 == f, pltpu.roll(a, 2 * f + 1, 1), edges)
    yh_send[...] = edges.T[: 2 * SUB]

    x_high, x_low = {"gx": lax.rem(ix + 1, dx)}, {"gx": lax.rem(ix + dx - 1, dx)}
    y_high, y_low = {"gy": lax.rem(iy + 1, dy)}, {"gy": lax.rem(iy + dy - 1, dy)}
    halos = [
        (copy(xh_send.at[0], xh_recv.at[0], hs.at[0], hr.at[0], x_high), ix < dx - 1, ix > 0),
        (copy(xh_send.at[1], xh_recv.at[1], hs.at[1], hr.at[1], x_low), ix > 0, ix < dx - 1),
        (copy(yh_send, yh_recv.at[0], hs.at[2], hr.at[2], y_high), iy < dy - 1, iy > 0),
        (copy(yh_send, yh_recv.at[1], hs.at[3], hr.at[3], y_low), iy > 0, iy < dy - 1),
    ]
    pl.semaphore_wait(barrier, dx + dy - 2)
    for c, sends, takes in halos:
        pl.when(sends)(c.start)
    for c, sends, takes in halos:
        pl.when(takes)(c.wait_recv)

    def low_row(f):
        return jnp.where(ix > 0, xh_recv[0, f : f + 1, :], 0.0)

    def high_row(f):
        return jnp.where(ix < dx - 1, xh_recv[1, f : f + 1, :], 0.0)

    first = [jnp.where(row == 0, low_row(nf + p), pltpu.roll(d[tx - 1, p], 1, 0)) for p in range(planes)]
    ax = 0.5 * (jnp.concatenate([jnp.stack(first)[None], d[:-1]], 0) + d)
    end = (row == SUB - 1) & (ix == dx - 1)
    gr = jnp.concatenate([jnp.ones_like(d[:-1]), (1.0 + jnp.where(end, 0.5 * d[tx - 1], 0.0))[None]], 0)
    xt, c, gl, gr = tree_matrix(ax, None, gr)
    xrow, c, gl, gr = rows_matrix(c, gl, gr)
    for p in range(planes):
        xg[ix, p : p + 1, :] = c[p, 7:8]
        xg[ix, planes + p : planes + p + 1, :] = gl[p, 7:8]
        xg[ix, 2 * planes + p : 2 * planes + p + 1, :] = gr[p, 7:8]

    take = lax.broadcasted_iota(jnp.int32, (2 * SUB, nx), 0) % 2 == 0
    halo = jnp.where(
        take, jnp.where(iy > 0, yh_recv[0], 0.0), jnp.where(iy < dy - 1, yh_recv[1], 0.0)
    )
    halo = jnp.concatenate([halo, jnp.zeros((ny - 2 * SUB, nx), jnp.float32)], 0).T

    def before_y(f):
        h = pltpu.roll(halo, ny - 2 * f - 1, 1)
        return h, pltpu.roll(jnp.where(lane == ny - 1, h, fields[f]), 1, 1)

    source = []
    for cc in range(ncomp):
        for p in range(planes):
            f = cc * planes + p
            a = v[:, cc, p]
            lo = jnp.where(row == 0, low_row(f), pltpu.roll(a[tx - 1], 1, 0))
            hi = jnp.where(row == SUB - 1, high_row(f), pltpu.roll(a[0], SUB - 1, 0))
            grad_x = jnp.concatenate([a[1:], hi[None]], 0) - jnp.concatenate([lo[None], a[:-1]], 0)
            h, prev = before_y(f)
            grad_y = pltpu.roll(jnp.where(lane == 0, h, fields[f]), ny - 1, 1) - prev
            grad_y = grad_y.reshape(tx, SUB, ny)
            source.append(a - (0.5 * courant) * (v[:, 0, p] * grad_x + v[:, 1, p] * grad_y))
    source = jnp.stack(source, 1).reshape(v.shape)
    xmids, il, ir = tree_source(None, source, xt, wide)
    xrowmids, il, ir = rows_source(il, ir, xrow)
    for f in range(nf):
        xg[ix, SUB + f : SUB + f + 1, :] = il[f // planes, f % planes, 7:8]
        xg[ix, 2 * SUB + f : 2 * SUB + f + 1, :] = ir[f // planes, f % planes, 7:8]
    x_copies = [
        copy(xg.at[ix], xg.at[ix], xs.at[o], xr.at[o], {"gx": peer})
        for o, peer in enumerate(x_peers)
    ]
    for c in x_copies:
        c.start()

    for p in range(planes):
        scr_d[p] = (0.5 * (before_y(nf + p)[1] + fields[nf + p])).T
    ay = jnp.stack([scr_d[:, pl.ds(t, SUB, stride=ty), :] for t in range(ty)])
    end = (row_y == SUB - 1) & (iy == dy - 1)
    last = [
        1.0 + jnp.where(end, 0.5 * yh_send[2 * (nf + p) : 2 * (nf + p) + 1, :], 0.0)
        for p in range(planes)
    ]
    gr = jnp.concatenate([jnp.ones_like(ay[:-1]), jnp.stack(last)[None]], 0)
    yt, c, gl, gr = tree_matrix(ay, None, gr)
    yrow, c, gl, gr = rows_matrix(c, gl, gr)
    for p in range(planes):
        ym[iy, p : p + 1, :] = c[p, 7:8]
        ym[iy, planes + p : planes + p + 1, :] = gl[p, 7:8]
        ym[iy, 2 * planes + p : 2 * planes + p + 1, :] = gr[p, 7:8]
    ym_copies = [
        copy(ym.at[iy], ym.at[iy], yms.at[o], ymr.at[o], {"gy": peer})
        for o, peer in enumerate(y_peers)
    ]
    for c in ym_copies:
        c.start()

    def same(a):
        return a

    def ends_matrix(tile):
        c, gl, gr = (spread(tile, k * planes) for k in range(3))
        levels, c, gl, gr = tree_matrix(c, gl, gr)
        return levels, 1.0 / (c + gr)

    def ends_solve(il, ir, levels, inverse, held, place):
        mids, il, ir = tree_source(il, ir, levels, same)
        held[0] = jnp.zeros(held.shape[1:], jnp.float32)
        held[1:] = tree_down(jnp.zeros_like(ir), ir * inverse, levels, mids, same)
        low, high = held[place], held[place + 1]

        def split(a):
            parts = [jnp.broadcast_to(a[f : f + 1], a.shape) for f in range(nf)]
            return jnp.stack(parts).reshape((ncomp, planes) + a.shape)

        return split(low), split(high)

    for c in x_copies:
        c.wait_recv()
    levels, inverse = ends_matrix(xg[:, :SUB])
    low, high = ends_solve(xg[:, SUB : 2 * SUB], xg[:, 2 * SUB :], levels, inverse, wx, ix)
    left, right = rows_down(low, high, xrow, xrowmids, row)
    middle = tree_down(left, right, xt, xmids, wide)

    for f in range(nf):
        cc, p = f // planes, f % planes
        scr[cc, p] = middle[:, cc, p].reshape(nx, ny).T
    m = jnp.stack([scr[:, :, pl.ds(t, SUB, stride=ty), :] for t in range(ty)])
    ymids, il, ir = tree_source(None, m, yt, wide)
    yrowmids, il, ir = rows_source(il, ir, yrow)
    for f in range(nf):
        yr[iy, f : f + 1, :] = il[f // planes, f % planes, 7:8]
        yr[iy, SUB + f : SUB + f + 1, :] = ir[f // planes, f % planes, 7:8]
    yr_copies = [
        copy(yr.at[iy], yr.at[iy], yrs.at[o], yrr.at[o], {"gy": peer})
        for o, peer in enumerate(y_peers)
    ]
    for c in yr_copies:
        c.start()

    for c in ym_copies:
        c.wait_recv()
    levels, inverse = ends_matrix(ym[...])
    for c in yr_copies:
        c.wait_recv()
    low, high = ends_solve(yr[:, :SUB], yr[:, SUB:], levels, inverse, wy, iy)
    left, right = rows_down(low, high, yrow, yrowmids, row_y)
    w = tree_down(left, right, yt, ymids, wide)
    for t in range(ty):
        scr[:, :, pl.ds(t, SUB, stride=ty), :] = w[t]
    for f in range(nf):
        cc, p = f // planes, f % planes
        a = scr[cc, p].T.reshape(tx, SUB, ny)
        for t in range(tx):
            out[cc, p, pl.ds(t, SUB, stride=tx), :] = a[t]

    for c, sends, takes in halos:
        pl.when(sends)(c.wait_send)
    for c in x_copies + ym_copies + yr_copies:
        c.wait_send()


def local(dx, dy, velocity, diffusion):
    ncomp, planes, nx, ny = velocity.shape
    vmem = pl.BlockSpec(memory_space=pltpu.VMEM)
    f32 = jnp.float32
    dma = pltpu.SemaphoreType.DMA
    return pl.pallas_call(
        functools.partial(kernel, dx, dy),
        out_shape=jax.ShapeDtypeStruct(velocity.shape, f32),
        in_specs=[vmem, vmem],
        out_specs=vmem,
        scratch_shapes=[
            pltpu.VMEM((2, SUB, ny), f32),
            pltpu.VMEM((2, SUB, ny), f32),
            pltpu.VMEM((2 * SUB, nx), f32),
            pltpu.VMEM((2, 2 * SUB, nx), f32),
            pltpu.VMEM((dx, 3 * SUB, ny), f32),
            pltpu.VMEM((dy, SUB, nx), f32),
            pltpu.VMEM((dy, 2 * SUB, nx), f32),
            pltpu.VMEM((dx + 1, SUB, ny), f32),
            pltpu.VMEM((dy + 1, SUB, nx), f32),
            pltpu.VMEM((ncomp, planes, ny, nx), f32),
            pltpu.VMEM((planes, ny, nx), f32),
            dma((4,)), dma((4,)),
            dma((dx,)), dma((dx,)),
            dma((dy,)), dma((dy,)),
            dma((dy,)), dma((dy,)),
        ],
        compiler_params=pltpu.CompilerParams(
            collective_id=0, has_side_effects=True, vmem_limit_bytes=48 * 1024 * 1024
        ),
    )(velocity, diffusion)


def solution(mesh):
    in_specs = (P(None, None, "gx", "gy"), P(None, "gx", "gy"))
    out_specs = P(None, None, "gx", "gy")
    body = functools.partial(local, mesh.shape["gx"], mesh.shape["gy"])
    return jax.shard_map(body, mesh=mesh, in_specs=in_specs, out_specs=out_specs, check_vma=False)
```

```python
import functools

import jax
import jax.numpy as jnp
from jax import lax
from jax.experimental import pallas as pl
from jax.experimental.pallas import tpu as pltpu
from jax.sharding import PartitionSpec as P

courant = 0.25
SUB = 8
MESH = pl.DeviceIdType.MESH


def halves(a):
    a = a.reshape((a.shape[0] // 2, 2) + a.shape[1:])
    return a[:, 0], a[:, 1]


def plus(a, b):
    return b if a is None else (a if b is None else a + b)


def join_matrix(c1, c2, gr1, gl2, gl1, gr2):
    g = gr1 + gl2
    r = 1.0 / (c1 + c2 + g)
    p, q = c1 * r, c2 * r
    return (p, q, r), p * c2, gl1 + p * g, gr2 + q * g


def tree_matrix(d, row):
    prev = jnp.concatenate([roll_rows(d[-1:], 1), d[:-1]], 0)
    c = 0.5 * (prev + d)
    kept = row == 0
    c1, c2 = halves(c)
    r = 1.0 / (c1 + c2 + 1.0)
    p, q = c1 * r, c2 * r
    p, q, r = (
        jnp.concatenate([jnp.where(kept, value, a[:1]), a[1:]], 0)
        for a, value in ((p, 1.0), (q, 0.0), (r, 0.0))
    )
    levels = [(p, q, r)]
    c, gl, gr = p * c2, p, 1.0 + q
    while c.shape[0] > 1:
        c1, c2 = halves(c)
        gr1, gr2 = halves(gr)
        gl1, gl2 = halves(gl)
        level, c, gl, gr = join_matrix(c1, c2, gr1, gl2, gl1, gr2)
        levels.append(level)
    return levels, c[0], gl[0], gr[0]


def tree_source(il, ir, levels, widen):
    mids = []
    for level in levels:
        p, q, r = (widen(a) for a in level)
        ir1, ir2 = halves(ir)
        il1, il2 = (None, None) if il is None else halves(il)
        i = plus(ir1, il2)
        mids.append(i * r)
        il = plus(il1, p * i)
        ir = ir2 + q * i
    return mids, il[0], ir[0]


def tree_down(left, right, levels, mids, widen):
    w = right[None]
    for level, mid in zip(reversed(levels), reversed(mids)):
        p, q = widen(level[0]), widen(level[1])
        wl = left[None] if w.shape[0] == 1 else jnp.concatenate([left[None], w[:-1]], 0)
        m = mid + p * wl + q * w
        w = jnp.stack([m, w], 1).reshape((2 * w.shape[0],) + w.shape[1:])
    return w


def roll_rows(a, shift):
    flat = a.reshape((-1,) + a.shape[-2:])
    out = [pltpu.roll(flat[k], shift % SUB, 0) for k in range(flat.shape[0])]
    return jnp.stack(out).reshape(a.shape)


def rows_matrix(c, gl, gr):
    levels = []
    for shift in (1, 2, 4):
        level, c, gl, gr = join_matrix(
            roll_rows(c, shift), c, roll_rows(gr, shift), gl, roll_rows(gl, shift), gr
        )
        levels.append(level)
    return levels, c, gl, gr


def rows_source(il, ir, levels):
    mids = []
    for shift, (p, q, r) in zip((1, 2, 4), levels):
        i = roll_rows(ir, shift) + il
        mids.append(i * r)
        il = roll_rows(il, shift) + p * i
        ir = ir + q * i
    return mids, il, ir


def rows_down(left, right, levels, mids, row):
    def solve(k, wl, wr):
        return mids[k] + levels[k][0] * wl + levels[k][1] * wr

    m = solve(2, left, right)
    m3 = jnp.broadcast_to(m[..., 7:8, :], m.shape)
    wr = jnp.where(row < 4, m3, right)
    m = solve(1, jnp.where(row < 4, left, m3), wr)
    m1 = jnp.broadcast_to(m[..., 3:4, :], m.shape)
    m5 = jnp.broadcast_to(m[..., 7:8, :], m.shape)
    wl = jnp.where(row < 2, left, jnp.where(row < 4, m1, jnp.where(row < 6, m3, m5)))
    wr = jnp.where(row < 2, m1, jnp.where(row < 4, m3, jnp.where(row < 6, m5, right)))
    m = solve(0, wl, wr)
    w = jnp.where(row % 2 == 1, wr, roll_rows(m, 7))
    return jnp.where(row == 0, left, roll_rows(w, 1)), w


def pick(place, items):
    out = items[0]
    for k in range(1, len(items)):
        out = jnp.where(place == k, items[k], out)
    return out


def tile_of(a, row):
    flat = a.reshape((-1,) + a.shape[-2:])
    out = jnp.zeros_like(flat[0])
    for f in range(flat.shape[0]):
        out = jnp.where(row == f, pltpu.roll(flat[f], (f + 1) % SUB, 0), out)
    return out


def put_matrix(ref, place, c, gl, gr, first, last):
    planes = c.shape[0]
    for p in range(planes):
        ref[place, p : p + 1, :] = c[p, SUB - 1 :]
        ref[place, planes + p : planes + p + 1, :] = gl[p, SUB - 1 :]
        ref[place, 2 * planes + p : 2 * planes + p + 1, :] = gr[p, SUB - 1 :]
        ref[place, 3 * planes + p : 3 * planes + p + 1, :] = first[p]
        ref[place, 4 * planes + p : 4 * planes + p + 1, :] = last[p]


def ends_matrix(ref, count, place, planes, row):
    def spread(k, quantity):
        return pick(
            row % planes,
            [ref[k, quantity * planes + p : quantity * planes + p + 1, :] for p in range(planes)],
        )

    c, gl, gr, first, last = ([spread(k, j) for k in range(count)] for j in range(5))
    link = [0.5 * (last[k - 1] + first[k]) if k else 0.5 * first[0] for k in range(count)]
    left, t_first, t_last = [gl[0] + link[0]], [], []
    right, u_first, u_last = [gr[-1] + 0.5 * last[-1]], [], []
    for k in range(count):
        t_first.append(c[k] / (c[k] + left[k]))
        g = gr[k] + t_first[k] * left[k]
        j = count - 1 - k
        u_last.insert(0, c[j] / (c[j] + right[0]))
        h = gl[j] + u_last[0] * right[0]
        if k < count - 1:
            t_last.append(link[k + 1] / (link[k + 1] + g))
            left.append(gl[k + 1] + t_last[k] * g)
            u_first.insert(0, link[j] / (link[j] + h))
            right.insert(0, gr[j - 1] + u_first[0] * h)
    u_first.insert(0, None)
    own_c, g, h = pick(place, c), pick(place, left), pick(place, right)
    r = 1.0 / (own_c * (g + h) + g * h)
    inner = ((own_c + h) * r, own_c * r, (own_c + g) * r)
    t_own, u_own = pick(place, t_first), pick(place, u_last)
    zero = jnp.zeros_like(own_c)
    from_first, from_last = [zero] * count, [zero] * count
    x = None
    for e in range(1, count):
        through = zero if x is None else x * t_first[e - 1] * t_last[e - 1]
        x = jnp.where(place == e - 1, t_last[e - 1], through)
        from_last[e], from_first[e] = x, x * t_own
    y = None
    for e in range(count - 2, -1, -1):
        through = zero if y is None else y * u_last[e + 1] * u_first[e + 1]
        y = jnp.where(place == e + 1, u_first[e + 1], through)
        from_first[e] = jnp.where(place > e, y, from_first[e])
        from_last[e] = jnp.where(place > e, y * u_own, from_last[e])
    return from_first, from_last, inner


def ends_send(send, il, ir, from_first, from_last, copies):
    for e in range(len(from_first)):
        send[e] = il * from_first[e] + ir * from_last[e]
    for c in copies:
        c.start()


def ends_solve(recv, il, ir, inner, count, place, ncomp, planes):
    for k in range(count):
        tile = recv[k]
        il = il + jnp.where(k < place, tile, 0.0)
        ir = ir + jnp.where(k > place, tile, 0.0)
    low = inner[0] * il + inner[1] * ir
    high = inner[1] * il + inner[2] * ir

    def split(a):
        parts = [jnp.broadcast_to(a[f : f + 1], a.shape) for f in range(ncomp * planes)]
        return jnp.stack(parts).reshape((ncomp, planes) + a.shape)

    return split(low), split(high)


def kernel(
    dx, dy, vel_in, dif_in, out,
    vel, dif, xh_send, xh_recv, yh_send, yh_recv,
    xm, ym, xr_send, xr_recv, yr_send, yr_recv, scr, scr_d,
    ins, hs, hr, xms, xmr, xs, xr, yms, ymr, ys, yr,
):
    ncomp, planes, nx, ny = vel.shape
    tx, ty = nx // SUB, ny // SUB
    nf = ncomp * planes
    ix, iy = lax.axis_index("gx"), lax.axis_index("gy")
    x_peers = [lax.rem(ix + o, dx) for o in range(1, dx)]
    y_peers = [lax.rem(iy + o, dy) for o in range(1, dy)]

    vel_copy = pltpu.make_async_copy(vel_in, vel, ins.at[0])
    dif_copy = pltpu.make_async_copy(dif_in, dif, ins.at[1])
    vel_copy.start()
    dif_copy.start()
    barrier = pltpu.get_barrier_semaphore()
    for peer in x_peers:
        pl.semaphore_signal(barrier, inc=1, device_id={"gx": peer}, device_id_type=MESH)
    for peer in y_peers:
        pl.semaphore_signal(barrier, inc=1, device_id={"gy": peer}, device_id_type=MESH)

    def copy(src, dst, send, recv, where):
        return pltpu.make_async_remote_copy(
            src_ref=src, dst_ref=dst, send_sem=send, recv_sem=recv,
            device_id=where, device_id_type=MESH,
        )

    def wide(a):
        return a[:, None]

    row = lax.broadcasted_iota(jnp.int32, (SUB, ny), 0)
    row_y = lax.broadcasted_iota(jnp.int32, (SUB, nx), 0)
    lane = lax.broadcasted_iota(jnp.int32, (nx, ny), 1)
    scale = 0.5 * courant

    vel_copy.wait()
    v = jnp.stack([vel[:, :, pl.ds(t, SUB, stride=tx), :] for t in range(tx)])
    fields = [v[:, c, p].reshape(nx, ny) for c in range(ncomp) for p in range(planes)]
    for f in range(nf):
        ref = vel.at[f // planes, f % planes]
        xh_send[0, f : f + 1, :] = ref[nx - 1 : nx, :]
        xh_send[1, f : f + 1, :] = ref[0:1, :]
    edges = jnp.zeros((nx, ny), jnp.float32)
    for f, a in enumerate(fields):
        edges = jnp.where(lane // 2 == f, pltpu.roll(a, 2 * f + 1, 1), edges)
    yh_send[...] = edges.T[: 2 * SUB]

    x_high, x_low = {"gx": lax.rem(ix + 1, dx)}, {"gx": lax.rem(ix + dx - 1, dx)}
    y_high, y_low = {"gy": lax.rem(iy + 1, dy)}, {"gy": lax.rem(iy + dy - 1, dy)}
    halos = [
        (copy(yh_send, yh_recv.at[0], hs.at[2], hr.at[2], y_high), iy < dy - 1, iy > 0),
        (copy(yh_send, yh_recv.at[1], hs.at[3], hr.at[3], y_low), iy > 0, iy < dy - 1),
        (copy(xh_send.at[0], xh_recv.at[0], hs.at[0], hr.at[0], x_high), ix < dx - 1, ix > 0),
        (copy(xh_send.at[1], xh_recv.at[1], hs.at[1], hr.at[1], x_low), ix > 0, ix < dx - 1),
    ]
    pl.semaphore_wait(barrier, dx + dy - 2)
    for c, sends, takes in halos:
        pl.when(sends)(c.start)

    dif_copy.wait()
    d = jnp.stack([dif[:, pl.ds(t, SUB, stride=tx), :] for t in range(tx)])
    xt, c, gl, gr = tree_matrix(d, row)
    xrow, c, gl, gr = rows_matrix(c, gl, gr)
    put_matrix(
        xm, ix, c, gl, gr, [dif[p, 0:1, :] for p in range(planes)],
        [dif[p, nx - 1 : nx, :] for p in range(planes)],
    )
    xm_copies = [
        copy(xm.at[ix], xm.at[ix], xms.at[o], xmr.at[o], {"gx": peer})
        for o, peer in enumerate(x_peers)
    ]
    for c in xm_copies:
        c.start()
    for p in range(planes):
        scr_d[p] = d[:, p].reshape(nx, ny).T
    dt = jnp.stack([scr_d[:, pl.ds(t, SUB, stride=ty), :] for t in range(ty)])
    yt, c, gl, gr = tree_matrix(dt, row_y)
    yrow, c, gl, gr = rows_matrix(c, gl, gr)
    put_matrix(
        ym, iy, c, gl, gr, [scr_d[p, 0:1, :] for p in range(planes)],
        [scr_d[p, ny - 1 : ny, :] for p in range(planes)],
    )
    ym_copies = [
        copy(ym.at[iy], ym.at[iy], yms.at[o], ymr.at[o], {"gy": peer})
        for o, peer in enumerate(y_peers)
    ]
    for c in ym_copies:
        c.start()

    source = []
    for cc in range(ncomp):
        for p in range(planes):
            f = cc * planes + p
            a = v[:, cc, p]
            lo = jnp.where(row == 0, 0.0, pltpu.roll(a[tx - 1], 1, 0))
            hi = jnp.where(row == SUB - 1, 0.0, pltpu.roll(a[0], SUB - 1, 0))
            grad_x = jnp.concatenate([a[1:], hi[None]], 0) - jnp.concatenate([lo[None], a[:-1]], 0)
            grad_y = jnp.where(lane == ny - 1, 0.0, pltpu.roll(fields[f], ny - 1, 1))
            grad_y = grad_y - jnp.where(lane == 0, 0.0, pltpu.roll(fields[f], 1, 1))
            grad_y = grad_y.reshape(tx, SUB, ny)
            source.append(a - scale * (v[:, 0, p] * grad_x + v[:, 1, p] * grad_y))
    side = jnp.where(lane == 0, scale, jnp.where(lane == ny - 1, -scale, 0.0))
    weight = [side * fields[planes + p] for p in range(planes)]

    for c in xm_copies:
        c.wait_recv()
    x_first, x_last, x_inner = ends_matrix(xm, dx, ix, planes, row)

    for c, sends, takes in halos:
        pl.when(takes)(c.wait_recv)
    take = lax.broadcasted_iota(jnp.int32, (2 * SUB, nx), 0) % 2 == 0
    halo = jnp.where(
        take,
        jnp.where(iy < dy - 1, pltpu.roll(yh_recv[1], 2 * SUB - 1, 0), 0.0),
        jnp.where(iy > 0, pltpu.roll(yh_recv[0], 1, 0), 0.0),
    )
    halo = jnp.where(lax.broadcasted_iota(jnp.int32, (2 * SUB, nx), 0) < 2 * nf, halo, 0.0)
    halo = jnp.concatenate([halo, jnp.zeros((ny - 2 * SUB, nx), jnp.float32)], 0).T
    for f in range(nf):
        near = pltpu.roll(halo, ny - 2 * f - 1, 1)
        source[f] = source[f] + (weight[f % planes] * near).reshape(tx, SUB, ny)
    source = jnp.stack(source, 1).reshape(v.shape)
    xmids, il, ir = tree_source(None, source, xt, wide)
    xrowmids, il, ir = rows_source(il, ir, xrow)
    own_first = pick(row % planes, [xh_send[1, p : p + 1, :] for p in range(planes)])
    own_last = pick(row % planes, [xh_send[0, p : p + 1, :] for p in range(planes)])
    il = tile_of(il, row) + scale * own_first * jnp.where(ix > 0, xh_recv[0], 0.0)
    ir = tile_of(ir, row) - scale * own_last * jnp.where(ix < dx - 1, xh_recv[1], 0.0)
    x_copies = [
        copy(xr_send.at[peer], xr_recv.at[ix], xs.at[o], xr.at[o], {"gx": peer})
        for o, peer in enumerate(x_peers)
    ]
    ends_send(xr_send, il, ir, x_first, x_last, x_copies)

    for c in ym_copies:
        c.wait_recv()
    y_first, y_last, y_inner = ends_matrix(ym, dy, iy, planes, row_y)

    for c in x_copies:
        c.wait_recv()
    low, high = ends_solve(xr_recv, il, ir, x_inner, dx, ix, ncomp, planes)
    left, right = rows_down(low, high, xrow, xrowmids, row)
    middle = tree_down(left, right, xt, xmids, wide)

    for f in range(nf):
        cc, p = f // planes, f % planes
        scr[cc, p] = middle[:, cc, p].reshape(nx, ny).T
    m = jnp.stack([scr[:, :, pl.ds(t, SUB, stride=ty), :] for t in range(ty)])
    ymids, il, ir = tree_source(None, m, yt, wide)
    yrowmids, il, ir = rows_source(il, ir, yrow)
    il, ir = tile_of(il, row_y), tile_of(ir, row_y)
    y_copies = [
        copy(yr_send.at[peer], yr_recv.at[iy], ys.at[o], yr.at[o], {"gy": peer})
        for o, peer in enumerate(y_peers)
    ]
    ends_send(yr_send, il, ir, y_first, y_last, y_copies)
    for c in y_copies:
        c.wait_recv()
    low, high = ends_solve(yr_recv, il, ir, y_inner, dy, iy, ncomp, planes)
    left, right = rows_down(low, high, yrow, yrowmids, row_y)
    w = tree_down(left, right, yt, ymids, wide)
    for t in range(ty):
        scr[:, :, pl.ds(t, SUB, stride=ty), :] = w[t]
    for f in range(nf):
        cc, p = f // planes, f % planes
        a = scr[cc, p].T.reshape(tx, SUB, ny)
        for t in range(tx):
            out[cc, p, pl.ds(t, SUB, stride=tx), :] = a[t]

    for c, sends, takes in halos:
        pl.when(sends)(c.wait_send)
    for c in xm_copies + ym_copies + x_copies + y_copies:
        c.wait_send()


def local(dx, dy, velocity, diffusion):
    ncomp, planes, nx, ny = velocity.shape
    vmem = pl.BlockSpec(memory_space=pltpu.VMEM)
    f32 = jnp.float32
    dma = pltpu.SemaphoreType.DMA
    return pl.pallas_call(
        functools.partial(kernel, dx, dy),
        out_shape=jax.ShapeDtypeStruct(velocity.shape, f32),
        in_specs=[pl.BlockSpec(memory_space=pl.ANY)] * 2,
        out_specs=vmem,
        scratch_shapes=[
            pltpu.VMEM(velocity.shape, f32),
            pltpu.VMEM(diffusion.shape, f32),
            pltpu.VMEM((2, SUB, ny), f32),
            pltpu.VMEM((2, SUB, ny), f32),
            pltpu.VMEM((2 * SUB, nx), f32),
            pltpu.VMEM((2, 2 * SUB, nx), f32),
            pltpu.VMEM((dx, 2 * SUB, ny), f32),
            pltpu.VMEM((dy, 2 * SUB, nx), f32),
            pltpu.VMEM((dx, SUB, ny), f32),
            pltpu.VMEM((dx, SUB, ny), f32),
            pltpu.VMEM((dy, SUB, nx), f32),
            pltpu.VMEM((dy, SUB, nx), f32),
            pltpu.VMEM((ncomp, planes, ny, nx), f32),
            pltpu.VMEM((planes, ny, nx), f32),
            dma((2,)), dma((4,)), dma((4,)),
            dma((dx,)), dma((dx,)), dma((dx,)), dma((dx,)),
            dma((dy,)), dma((dy,)), dma((dy,)), dma((dy,)),
        ],
        compiler_params=pltpu.CompilerParams(
            collective_id=0, has_side_effects=True, vmem_limit_bytes=60 * 1024 * 1024
        ),
    )(velocity, diffusion)


def solution(mesh):
    in_specs = (P(None, None, "gx", "gy"), P(None, "gx", "gy"))
    out_specs = P(None, None, "gx", "gy")
    body = functools.partial(local, mesh.shape["gx"], mesh.shape["gy"])
    return jax.shard_map(body, mesh=mesh, in_specs=in_specs, out_specs=out_specs, check_vma=False)
```

```python
import functools

import jax
import jax.numpy as jnp
from jax import lax
from jax.experimental import pallas as pl
from jax.experimental.pallas import tpu as pltpu
from jax.sharding import PartitionSpec as P

courant = 0.25
SUB = 8
MESH = pl.DeviceIdType.MESH


def halves(a):
    a = a.reshape((a.shape[0] // 2, 2) + a.shape[1:])
    return a[:, 0], a[:, 1]


def plus(a, b):
    return b if a is None else (a if b is None else a + b)


def join_matrix(c1, c2, gr1, gl2, gl1, gr2):
    g = gr1 + gl2
    r = 1.0 / (c1 + c2 + g)
    p, q = c1 * r, c2 * r
    return (p, q, r), p * c2, gl1 + p * g, gr2 + q * g


def tree_matrix(d, row):
    prev = jnp.concatenate([roll_rows(d[-1:], 1), d[:-1]], 0)
    c = 0.5 * (prev + d)
    kept = row == 0
    c1, c2 = halves(c)
    r = 1.0 / (c1 + c2 + 1.0)
    p, q = c1 * r, c2 * r
    p, q, r = (
        jnp.concatenate([jnp.where(kept, value, a[:1]), a[1:]], 0)
        for a, value in ((p, 1.0), (q, 0.0), (r, 0.0))
    )
    levels = [(p, q, r)]
    c, gl, gr = p * c2, p, 1.0 + q
    while c.shape[0] > 1:
        c1, c2 = halves(c)
        gr1, gr2 = halves(gr)
        gl1, gl2 = halves(gl)
        level, c, gl, gr = join_matrix(c1, c2, gr1, gl2, gl1, gr2)
        levels.append(level)
    return levels, c[0], gl[0], gr[0]


def tree_source(il, ir, levels, widen):
    mids = []
    for level in levels:
        p, q, r = (widen(a) for a in level)
        ir1, ir2 = halves(ir)
        il1, il2 = (None, None) if il is None else halves(il)
        i = plus(ir1, il2)
        mids.append(i * r)
        il = plus(il1, p * i)
        ir = ir2 + q * i
    return mids, il[0], ir[0]


def tree_down(left, right, levels, mids, widen):
    w = right[None]
    for level, mid in zip(reversed(levels), reversed(mids)):
        p, q = widen(level[0]), widen(level[1])
        wl = left[None] if w.shape[0] == 1 else jnp.concatenate([left[None], w[:-1]], 0)
        m = mid + p * wl + q * w
        w = jnp.stack([m, w], 1).reshape((2 * w.shape[0],) + w.shape[1:])
    return w


def roll_rows(a, shift):
    flat = a.reshape((-1,) + a.shape[-2:])
    out = [pltpu.roll(flat[k], shift % SUB, 0) for k in range(flat.shape[0])]
    return jnp.stack(out).reshape(a.shape)


def rows_matrix(c, gl, gr):
    levels = []
    for shift in (1, 2, 4):
        level, c, gl, gr = join_matrix(
            roll_rows(c, shift), c, roll_rows(gr, shift), gl, roll_rows(gl, shift), gr
        )
        levels.append(level)
    return levels, c, gl, gr


def rows_source(il, ir, levels):
    mids = []
    for shift, (p, q, r) in zip((1, 2, 4), levels):
        i = roll_rows(ir, shift) + il
        mids.append(i * r)
        il = roll_rows(il, shift) + p * i
        ir = ir + q * i
    return mids, il, ir


def rows_down(left, right, levels, mids, row):
    def solve(k, wl, wr):
        return mids[k] + levels[k][0] * wl + levels[k][1] * wr

    m = solve(2, left, right)
    m3 = jnp.broadcast_to(m[..., 7:8, :], m.shape)
    wr = jnp.where(row < 4, m3, right)
    m = solve(1, jnp.where(row < 4, left, m3), wr)
    m1 = jnp.broadcast_to(m[..., 3:4, :], m.shape)
    m5 = jnp.broadcast_to(m[..., 7:8, :], m.shape)
    wl = jnp.where(row < 2, left, jnp.where(row < 4, m1, jnp.where(row < 6, m3, m5)))
    wr = jnp.where(row < 2, m1, jnp.where(row < 4, m3, jnp.where(row < 6, m5, right)))
    m = solve(0, wl, wr)
    w = jnp.where(row % 2 == 1, wr, roll_rows(m, 7))
    return jnp.where(row == 0, left, roll_rows(w, 1)), w


def pick(place, items):
    out = items[0]
    for k in range(1, len(items)):
        out = jnp.where(place == k, items[k], out)
    return out


def tile_of(a, row):
    flat = a.reshape((-1,) + a.shape[-2:])
    out = jnp.zeros_like(flat[0])
    for f in range(flat.shape[0]):
        out = jnp.where(row == f, pltpu.roll(flat[f], (f + 1) % SUB, 0), out)
    return out


def put_matrix(ref, place, c, gl, gr, first, last):
    planes = c.shape[0]
    for p in range(planes):
        ref[place, p : p + 1, :] = c[p, SUB - 1 :]
        ref[place, planes + p : planes + p + 1, :] = gl[p, SUB - 1 :]
        ref[place, 2 * planes + p : 2 * planes + p + 1, :] = gr[p, SUB - 1 :]
        ref[place, 3 * planes + p : 3 * planes + p + 1, :] = first[p]
        ref[place, 4 * planes + p : 4 * planes + p + 1, :] = last[p]


def ends_matrix(ref, count, place, planes, row):
    def spread(k, quantity):
        return pick(
            row % planes,
            [ref[k, quantity * planes + p : quantity * planes + p + 1, :] for p in range(planes)],
        )

    c, gl, gr, first, last = ([spread(k, j) for k in range(count)] for j in range(5))
    link = [0.5 * (last[k - 1] + first[k]) if k else 0.5 * first[0] for k in range(count)]
    left, t_first, t_last = [gl[0] + link[0]], [], []
    right, u_first, u_last = [gr[-1] + 0.5 * last[-1]], [], []
    for k in range(count):
        t_first.append(c[k] / (c[k] + left[k]))
        g = gr[k] + t_first[k] * left[k]
        j = count - 1 - k
        u_last.insert(0, c[j] / (c[j] + right[0]))
        h = gl[j] + u_last[0] * right[0]
        if k < count - 1:
            t_last.append(link[k + 1] / (link[k + 1] + g))
            left.append(gl[k + 1] + t_last[k] * g)
            u_first.insert(0, link[j] / (link[j] + h))
            right.insert(0, gr[j - 1] + u_first[0] * h)
    u_first.insert(0, None)
    own_c, g, h = pick(place, c), pick(place, left), pick(place, right)
    r = 1.0 / (own_c * (g + h) + g * h)
    inner = ((own_c + h) * r, own_c * r, (own_c + g) * r)
    t_own, u_own = pick(place, t_first), pick(place, u_last)
    zero = jnp.zeros_like(own_c)
    from_first, from_last = [zero] * count, [zero] * count
    x = None
    for e in range(1, count):
        through = zero if x is None else x * t_first[e - 1] * t_last[e - 1]
        x = jnp.where(place == e - 1, t_last[e - 1], through)
        from_last[e], from_first[e] = x, x * t_own
    y = None
    for e in range(count - 2, -1, -1):
        through = zero if y is None else y * u_last[e + 1] * u_first[e + 1]
        y = jnp.where(place == e + 1, u_first[e + 1], through)
        from_first[e] = jnp.where(place > e, y, from_first[e])
        from_last[e] = jnp.where(place > e, y * u_own, from_last[e])
    return from_first, from_last, inner


def ends_send(send, il, ir, from_first, from_last, copies):
    for e in range(len(from_first)):
        send[e] = il * from_first[e] + ir * from_last[e]
    for c in copies:
        c.start()


def ends_solve(recv, il, ir, inner, count, place, ncomp, planes):
    for k in range(count):
        tile = recv[k]
        il = il + jnp.where(k < place, tile, 0.0)
        ir = ir + jnp.where(k > place, tile, 0.0)
    low = inner[0] * il + inner[1] * ir
    high = inner[1] * il + inner[2] * ir

    def split(a):
        parts = [jnp.broadcast_to(a[f : f + 1], a.shape) for f in range(ncomp * planes)]
        return jnp.stack(parts).reshape((ncomp, planes) + a.shape)

    return split(low), split(high)


def kernel(
    dx, dy, vel_in, dif, out,
    vel, xh_send, xh_recv, yh_send, yh_recv,
    xm, ym, xr_send, xr_recv, yr_send, yr_recv, scr, scr_d,
    ins, hs, hr, xms, xmr, xs, xr, yms, ymr, ys, yr,
):
    ncomp, planes, nx, ny = vel.shape
    tx, ty = nx // SUB, ny // SUB
    nf = ncomp * planes
    ix, iy = lax.axis_index("gx"), lax.axis_index("gy")
    x_peers = [lax.rem(ix + o, dx) for o in range(1, dx)]
    y_peers = [lax.rem(iy + o, dy) for o in range(1, dy)]

    vel_copy = pltpu.make_async_copy(vel_in, vel, ins.at[0])
    vel_copy.start()
    barrier = pltpu.get_barrier_semaphore()
    for peer in x_peers:
        pl.semaphore_signal(barrier, inc=1, device_id={"gx": peer}, device_id_type=MESH)
    for peer in y_peers:
        pl.semaphore_signal(barrier, inc=1, device_id={"gy": peer}, device_id_type=MESH)

    def copy(src, dst, send, recv, where):
        return pltpu.make_async_remote_copy(
            src_ref=src, dst_ref=dst, send_sem=send, recv_sem=recv,
            device_id=where, device_id_type=MESH,
        )

    def wide(a):
        return a[:, None]

    row = lax.broadcasted_iota(jnp.int32, (SUB, ny), 0)
    row_y = lax.broadcasted_iota(jnp.int32, (SUB, nx), 0)
    lane = lax.broadcasted_iota(jnp.int32, (nx, ny), 1)
    scale = 0.5 * courant

    d = jnp.stack([dif[:, pl.ds(t, SUB, stride=tx), :] for t in range(tx)])
    xt, c, gl, gr = tree_matrix(d, row)
    xrow, c, gl, gr = rows_matrix(c, gl, gr)
    put_matrix(
        xm, ix, c, gl, gr, [dif[p, 0:1, :] for p in range(planes)],
        [dif[p, nx - 1 : nx, :] for p in range(planes)],
    )
    for p in range(planes):
        scr_d[p] = d[:, p].reshape(nx, ny).T
    dt = jnp.stack([scr_d[:, pl.ds(t, SUB, stride=ty), :] for t in range(ty)])
    yt, c, gl, gr = tree_matrix(dt, row_y)
    yrow, c, gl, gr = rows_matrix(c, gl, gr)
    put_matrix(
        ym, iy, c, gl, gr, [scr_d[p, 0:1, :] for p in range(planes)],
        [scr_d[p, ny - 1 : ny, :] for p in range(planes)],
    )

    vel_copy.wait()
    v = jnp.stack([vel[:, :, pl.ds(t, SUB, stride=tx), :] for t in range(tx)])
    fields = [v[:, c, p].reshape(nx, ny) for c in range(ncomp) for p in range(planes)]
    for f in range(nf):
        ref = vel.at[f // planes, f % planes]
        xh_send[0, f : f + 1, :] = ref[nx - 1 : nx, :]
        xh_send[1, f : f + 1, :] = ref[0:1, :]
    edges = jnp.zeros((nx, ny), jnp.float32)
    for f, a in enumerate(fields):
        edges = jnp.where(lane // 2 == f, pltpu.roll(a, 2 * f + 1, 1), edges)
    yh_send[...] = edges.T[: 2 * SUB]

    x_high, x_low = {"gx": lax.rem(ix + 1, dx)}, {"gx": lax.rem(ix + dx - 1, dx)}
    y_high, y_low = {"gy": lax.rem(iy + 1, dy)}, {"gy": lax.rem(iy + dy - 1, dy)}
    halos = [
        (copy(yh_send, yh_recv.at[0], hs.at[2], hr.at[2], y_high), iy < dy - 1, iy > 0),
        (copy(yh_send, yh_recv.at[1], hs.at[3], hr.at[3], y_low), iy > 0, iy < dy - 1),
        (copy(xh_send.at[0], xh_recv.at[0], hs.at[0], hr.at[0], x_high), ix < dx - 1, ix > 0),
        (copy(xh_send.at[1], xh_recv.at[1], hs.at[1], hr.at[1], x_low), ix > 0, ix < dx - 1),
    ]
    pl.semaphore_wait(barrier, dx + dy - 2)
    for c, sends, takes in halos:
        pl.when(sends)(c.start)

    xm_copies = [
        copy(xm.at[ix], xm.at[ix], xms.at[o], xmr.at[o], {"gx": peer})
        for o, peer in enumerate(x_peers)
    ]
    for c in xm_copies:
        c.start()
    ym_copies = [
        copy(ym.at[iy], ym.at[iy], yms.at[o], ymr.at[o], {"gy": peer})
        for o, peer in enumerate(y_peers)
    ]
    for c in ym_copies:
        c.start()

    source = []
    for cc in range(ncomp):
        for p in range(planes):
            f = cc * planes + p
            a = v[:, cc, p]
            lo = jnp.where(row == 0, 0.0, pltpu.roll(a[tx - 1], 1, 0))
            hi = jnp.where(row == SUB - 1, 0.0, pltpu.roll(a[0], SUB - 1, 0))
            grad_x = jnp.concatenate([a[1:], hi[None]], 0) - jnp.concatenate([lo[None], a[:-1]], 0)
            grad_y = jnp.where(lane == ny - 1, 0.0, pltpu.roll(fields[f], ny - 1, 1))
            grad_y = grad_y - jnp.where(lane == 0, 0.0, pltpu.roll(fields[f], 1, 1))
            grad_y = grad_y.reshape(tx, SUB, ny)
            source.append(a - scale * (v[:, 0, p] * grad_x + v[:, 1, p] * grad_y))
    side = jnp.where(lane == 0, scale, jnp.where(lane == ny - 1, -scale, 0.0))
    weight = [side * fields[planes + p] for p in range(planes)]

    for c in xm_copies:
        c.wait_recv()
    x_first, x_last, x_inner = ends_matrix(xm, dx, ix, planes, row)

    for c, sends, takes in halos:
        pl.when(takes)(c.wait_recv)
    take = lax.broadcasted_iota(jnp.int32, (2 * SUB, nx), 0) % 2 == 0
    halo = jnp.where(
        take,
        jnp.where(iy < dy - 1, pltpu.roll(yh_recv[1], 2 * SUB - 1, 0), 0.0),
        jnp.where(iy > 0, pltpu.roll(yh_recv[0], 1, 0), 0.0),
    )
    halo = jnp.where(lax.broadcasted_iota(jnp.int32, (2 * SUB, nx), 0) < 2 * nf, halo, 0.0)
    halo = jnp.concatenate([halo, jnp.zeros((ny - 2 * SUB, nx), jnp.float32)], 0).T
    for f in range(nf):
        near = pltpu.roll(halo, ny - 2 * f - 1, 1)
        source[f] = source[f] + (weight[f % planes] * near).reshape(tx, SUB, ny)
    source = jnp.stack(source, 1).reshape(v.shape)
    xmids, il, ir = tree_source(None, source, xt, wide)
    xrowmids, il, ir = rows_source(il, ir, xrow)
    own_first = pick(row % planes, [xh_send[1, p : p + 1, :] for p in range(planes)])
    own_last = pick(row % planes, [xh_send[0, p : p + 1, :] for p in range(planes)])
    il = tile_of(il, row) + scale * own_first * jnp.where(ix > 0, xh_recv[0], 0.0)
    ir = tile_of(ir, row) - scale * own_last * jnp.where(ix < dx - 1, xh_recv[1], 0.0)
    x_copies = [
        copy(xr_send.at[peer], xr_recv.at[ix], xs.at[o], xr.at[o], {"gx": peer})
        for o, peer in enumerate(x_peers)
    ]
    ends_send(xr_send, il, ir, x_first, x_last, x_copies)

    for c in ym_copies:
        c.wait_recv()
    y_first, y_last, y_inner = ends_matrix(ym, dy, iy, planes, row_y)

    for c in x_copies:
        c.wait_recv()
    low, high = ends_solve(xr_recv, il, ir, x_inner, dx, ix, ncomp, planes)
    left, right = rows_down(low, high, xrow, xrowmids, row)
    middle = tree_down(left, right, xt, xmids, wide)

    for f in range(nf):
        cc, p = f // planes, f % planes
        scr[cc, p] = middle[:, cc, p].reshape(nx, ny).T
    m = jnp.stack([scr[:, :, pl.ds(t, SUB, stride=ty), :] for t in range(ty)])
    ymids, il, ir = tree_source(None, m, yt, wide)
    yrowmids, il, ir = rows_source(il, ir, yrow)
    il, ir = tile_of(il, row_y), tile_of(ir, row_y)
    y_copies = [
        copy(yr_send.at[peer], yr_recv.at[iy], ys.at[o], yr.at[o], {"gy": peer})
        for o, peer in enumerate(y_peers)
    ]
    ends_send(yr_send, il, ir, y_first, y_last, y_copies)
    for c in y_copies:
        c.wait_recv()
    low, high = ends_solve(yr_recv, il, ir, y_inner, dy, iy, ncomp, planes)
    left, right = rows_down(low, high, yrow, yrowmids, row_y)
    w = tree_down(left, right, yt, ymids, wide)
    for t in range(ty):
        scr[:, :, pl.ds(t, SUB, stride=ty), :] = w[t]
    for f in range(nf):
        cc, p = f // planes, f % planes
        a = scr[cc, p].T.reshape(tx, SUB, ny)
        for t in range(tx):
            out[cc, p, pl.ds(t, SUB, stride=tx), :] = a[t]

    for c, sends, takes in halos:
        pl.when(sends)(c.wait_send)
    for c in xm_copies + ym_copies + x_copies + y_copies:
        c.wait_send()


def local(dx, dy, velocity, diffusion):
    ncomp, planes, nx, ny = velocity.shape
    vmem = pl.BlockSpec(memory_space=pltpu.VMEM)
    f32 = jnp.float32
    dma = pltpu.SemaphoreType.DMA
    return pl.pallas_call(
        functools.partial(kernel, dx, dy),
        out_shape=jax.ShapeDtypeStruct(velocity.shape, f32),
        in_specs=[pl.BlockSpec(memory_space=pl.ANY), vmem],
        out_specs=vmem,
        scratch_shapes=[
            pltpu.VMEM(velocity.shape, f32),
            pltpu.VMEM((2, SUB, ny), f32),
            pltpu.VMEM((2, SUB, ny), f32),
            pltpu.VMEM((2 * SUB, nx), f32),
            pltpu.VMEM((2, 2 * SUB, nx), f32),
            pltpu.VMEM((dx, 2 * SUB, ny), f32),
            pltpu.VMEM((dy, 2 * SUB, nx), f32),
            pltpu.VMEM((dx, SUB, ny), f32),
            pltpu.VMEM((dx, SUB, ny), f32),
            pltpu.VMEM((dy, SUB, nx), f32),
            pltpu.VMEM((dy, SUB, nx), f32),
            pltpu.VMEM((ncomp, planes, ny, nx), f32),
            pltpu.VMEM((planes, ny, nx), f32),
            dma((1,)), dma((4,)), dma((4,)),
            dma((dx,)), dma((dx,)), dma((dx,)), dma((dx,)),
            dma((dy,)), dma((dy,)), dma((dy,)), dma((dy,)),
        ],
        compiler_params=pltpu.CompilerParams(
            collective_id=0, has_side_effects=True, vmem_limit_bytes=54592 * 1024
        ),
    )(velocity, diffusion)


def solution(mesh):
    in_specs = (P(None, None, "gx", "gy"), P(None, "gx", "gy"))
    out_specs = P(None, None, "gx", "gy")
    body = functools.partial(local, mesh.shape["gx"], mesh.shape["gy"])
    return jax.shard_map(body, mesh=mesh, in_specs=in_specs, out_specs=out_specs, check_vma=False)
```

```python
import functools

import jax
import jax.numpy as jnp
from jax import lax
from jax.experimental import pallas as pl
from jax.experimental.pallas import tpu as pltpu
from jax.sharding import PartitionSpec as P

courant = 0.25
SUB = 8
MESH = pl.DeviceIdType.MESH


def halves(a):
    a = a.reshape((a.shape[0] // 2, 2) + a.shape[1:])
    return a[:, 0], a[:, 1]


def plus(a, b):
    return b if a is None else (a if b is None else a + b)


def join_matrix(c1, c2, gr1, gl2, gl1, gr2):
    g = gr1 + gl2
    r = 1.0 / (c1 + c2 + g)
    p, q = c1 * r, c2 * r
    return (p, q, r), p * c2, gl1 + p * g, gr2 + q * g


def tree_matrix(d, row):
    prev = jnp.concatenate([roll_rows(d[-1:], 1), d[:-1]], 0)
    c = 0.5 * (prev + d)
    kept = row == 0
    c1, c2 = halves(c)
    r = 1.0 / (c1 + c2 + 1.0)
    p, q = c1 * r, c2 * r
    p, q, r = (
        jnp.concatenate([jnp.where(kept, value, a[:1]), a[1:]], 0)
        for a, value in ((p, 1.0), (q, 0.0), (r, 0.0))
    )
    levels = [(p, q, r)]
    c, gl, gr = p * c2, p, 1.0 + q
    while c.shape[0] > 1:
        c1, c2 = halves(c)
        gr1, gr2 = halves(gr)
        gl1, gl2 = halves(gl)
        level, c, gl, gr = join_matrix(c1, c2, gr1, gl2, gl1, gr2)
        levels.append(level)
    return levels, c[0], gl[0], gr[0]


def tree_source(il, ir, levels, widen):
    mids = []
    for level in levels:
        p, q, r = (widen(a) for a in level)
        ir1, ir2 = halves(ir)
        il1, il2 = (None, None) if il is None else halves(il)
        i = plus(ir1, il2)
        mids.append(i * r)
        il = plus(il1, p * i)
        ir = ir2 + q * i
    return mids, il[0], ir[0]


def tree_down(left, right, levels, mids, widen):
    w = right[None]
    for level, mid in zip(reversed(levels), reversed(mids)):
        p, q = widen(level[0]), widen(level[1])
        wl = left[None] if w.shape[0] == 1 else jnp.concatenate([left[None], w[:-1]], 0)
        m = mid + p * wl + q * w
        w = jnp.stack([m, w], 1).reshape((2 * w.shape[0],) + w.shape[1:])
    return w


def roll_rows(a, shift):
    flat = a.reshape((-1,) + a.shape[-2:])
    out = [pltpu.roll(flat[k], shift % SUB, 0) for k in range(flat.shape[0])]
    return jnp.stack(out).reshape(a.shape)


def rows_matrix(c, gl, gr):
    levels = []
    for shift in (1, 2, 4):
        level, c, gl, gr = join_matrix(
            roll_rows(c, shift), c, roll_rows(gr, shift), gl, roll_rows(gl, shift), gr
        )
        levels.append(level)
    return levels, c, gl, gr


def rows_source(il, ir, levels):
    mids = []
    for shift, (p, q, r) in zip((1, 2, 4), levels):
        i = roll_rows(ir, shift) + il
        mids.append(i * r)
        il = roll_rows(il, shift) + p * i
        ir = ir + q * i
    return mids, il, ir


def rows_down(left, right, levels, mids, row):
    def solve(k, wl, wr):
        return mids[k] + levels[k][0] * wl + levels[k][1] * wr

    m = solve(2, left, right)
    m3 = jnp.broadcast_to(m[..., 7:8, :], m.shape)
    wr = jnp.where(row < 4, m3, right)
    m = solve(1, jnp.where(row < 4, left, m3), wr)
    m1 = jnp.broadcast_to(m[..., 3:4, :], m.shape)
    m5 = jnp.broadcast_to(m[..., 7:8, :], m.shape)
    wl = jnp.where(row < 2, left, jnp.where(row < 4, m1, jnp.where(row < 6, m3, m5)))
    wr = jnp.where(row < 2, m1, jnp.where(row < 4, m3, jnp.where(row < 6, m5, right)))
    m = solve(0, wl, wr)
    w = jnp.where(row % 2 == 1, wr, roll_rows(m, 7))
    return jnp.where(row == 0, left, roll_rows(w, 1)), w


def pick(place, items):
    out = items[0]
    for k in range(1, len(items)):
        out = jnp.where(place == k, items[k], out)
    return out


def tile_of(a, row):
    flat = a.reshape((-1,) + a.shape[-2:])
    out = jnp.zeros_like(flat[0])
    for f in range(flat.shape[0]):
        out = jnp.where(row == f, pltpu.roll(flat[f], (f + 1) % SUB, 0), out)
    return out


def put_matrix(ref, place, c, gl, gr, first, last):
    planes = c.shape[0]
    for p in range(planes):
        ref[place, p : p + 1, :] = c[p, SUB - 1 :]
        ref[place, planes + p : planes + p + 1, :] = gl[p, SUB - 1 :]
        ref[place, 2 * planes + p : 2 * planes + p + 1, :] = gr[p, SUB - 1 :]
        ref[place, 3 * planes + p : 3 * planes + p + 1, :] = first[p]
        ref[place, 4 * planes + p : 4 * planes + p + 1, :] = last[p]


def ends_matrix(ref, count, place, planes, row):
    def spread(k, quantity):
        return pick(
            row % planes,
            [ref[k, quantity * planes + p : quantity * planes + p + 1, :] for p in range(planes)],
        )

    c, gl, gr, first, last = ([spread(k, j) for k in range(count)] for j in range(5))
    link = [0.5 * (last[k - 1] + first[k]) if k else 0.5 * first[0] for k in range(count)]
    left, t_first, t_last = [gl[0] + link[0]], [], []
    right, u_first, u_last = [gr[-1] + 0.5 * last[-1]], [], []
    for k in range(count):
        t_first.append(c[k] / (c[k] + left[k]))
        g = gr[k] + t_first[k] * left[k]
        j = count - 1 - k
        u_last.insert(0, c[j] / (c[j] + right[0]))
        h = gl[j] + u_last[0] * right[0]
        if k < count - 1:
            t_last.append(link[k + 1] / (link[k + 1] + g))
            left.append(gl[k + 1] + t_last[k] * g)
            u_first.insert(0, link[j] / (link[j] + h))
            right.insert(0, gr[j - 1] + u_first[0] * h)
    u_first.insert(0, None)
    own_c, g, h = pick(place, c), pick(place, left), pick(place, right)
    r = 1.0 / (own_c * (g + h) + g * h)
    inner = ((own_c + h) * r, own_c * r, (own_c + g) * r)
    t_own, u_own = pick(place, t_first), pick(place, u_last)
    zero = jnp.zeros_like(own_c)
    from_first, from_last = [zero] * count, [zero] * count
    x = None
    for e in range(1, count):
        through = zero if x is None else x * t_first[e - 1] * t_last[e - 1]
        x = jnp.where(place == e - 1, t_last[e - 1], through)
        from_last[e], from_first[e] = x, x * t_own
    y = None
    for e in range(count - 2, -1, -1):
        through = zero if y is None else y * u_last[e + 1] * u_first[e + 1]
        y = jnp.where(place == e + 1, u_first[e + 1], through)
        from_first[e] = jnp.where(place > e, y, from_first[e])
        from_last[e] = jnp.where(place > e, y * u_own, from_last[e])
    return from_first, from_last, inner


def ends_send(send, il, ir, from_first, from_last, copies):
    for e in range(len(from_first)):
        send[e] = il * from_first[e] + ir * from_last[e]
    for c in copies:
        c.start()


def ends_solve(recv, il, ir, inner, count, place, ncomp, planes):
    for k in range(count):
        tile = recv[k]
        il = il + jnp.where(k < place, tile, 0.0)
        ir = ir + jnp.where(k > place, tile, 0.0)
    low = inner[0] * il + inner[1] * ir
    high = inner[1] * il + inner[2] * ir

    def split(a):
        parts = [jnp.broadcast_to(a[f : f + 1], a.shape) for f in range(ncomp * planes)]
        return jnp.stack(parts).reshape((ncomp, planes) + a.shape)

    return split(low), split(high)


def kernel(
    dx, dy, vel_in, dif, out,
    vel, xh_send, xh_recv, yh_send, yh_recv,
    xm, ym, xr_send, xr_recv, yr_send, yr_recv, scr, scr_d,
    ins, hs, hr, xms, xmr, xs, xr, yms, ymr, ys, yr,
):
    ncomp, planes, nx, ny = vel.shape
    tx, ty = nx // SUB, ny // SUB
    nf = ncomp * planes
    ix, iy = lax.axis_index("gx"), lax.axis_index("gy")
    x_peers = [lax.rem(ix + o, dx) for o in range(1, dx)]
    y_peers = [lax.rem(iy + o, dy) for o in range(1, dy)]

    vel_copy = pltpu.make_async_copy(vel_in, vel, ins.at[0])
    vel_copy.start()
    barrier = pltpu.get_barrier_semaphore()
    for peer in x_peers:
        pl.semaphore_signal(barrier, inc=1, device_id={"gx": peer}, device_id_type=MESH)
    for peer in y_peers:
        pl.semaphore_signal(barrier, inc=1, device_id={"gy": peer}, device_id_type=MESH)

    def copy(src, dst, send, recv, where):
        return pltpu.make_async_remote_copy(
            src_ref=src, dst_ref=dst, send_sem=send, recv_sem=recv,
            device_id=where, device_id_type=MESH,
        )

    def wide(a):
        return a[:, None]

    row = lax.broadcasted_iota(jnp.int32, (SUB, ny), 0)
    row_y = lax.broadcasted_iota(jnp.int32, (SUB, nx), 0)
    lane = lax.broadcasted_iota(jnp.int32, (nx, ny), 1)
    scale = 0.5 * courant

    d = jnp.stack([dif[:, pl.ds(t, SUB, stride=tx), :] for t in range(tx)])
    xt, c, gl, gr = tree_matrix(d, row)
    xrow, c, gl, gr = rows_matrix(c, gl, gr)
    put_matrix(
        xm, ix, c, gl, gr, [dif[p, 0:1, :] for p in range(planes)],
        [dif[p, nx - 1 : nx, :] for p in range(planes)],
    )

    vel_copy.wait()
    v = jnp.stack([vel[:, :, pl.ds(t, SUB, stride=tx), :] for t in range(tx)])
    fields = [v[:, c, p].reshape(nx, ny) for c in range(ncomp) for p in range(planes)]
    for f in range(nf):
        ref = vel.at[f // planes, f % planes]
        xh_send[0, f : f + 1, :] = ref[nx - 1 : nx, :]
        xh_send[1, f : f + 1, :] = ref[0:1, :]
    edges = jnp.zeros((nx, ny), jnp.float32)
    for f, a in enumerate(fields):
        edges = jnp.where(lane // 2 == f, pltpu.roll(a, 2 * f + 1, 1), edges)
    yh_send[...] = edges.T[: 2 * SUB]

    x_high, x_low = {"gx": lax.rem(ix + 1, dx)}, {"gx": lax.rem(ix + dx - 1, dx)}
    y_high, y_low = {"gy": lax.rem(iy + 1, dy)}, {"gy": lax.rem(iy + dy - 1, dy)}
    halos = [
        (copy(yh_send, yh_recv.at[0], hs.at[2], hr.at[2], y_high), iy < dy - 1, iy > 0),
        (copy(yh_send, yh_recv.at[1], hs.at[3], hr.at[3], y_low), iy > 0, iy < dy - 1),
        (copy(xh_send.at[0], xh_recv.at[0], hs.at[0], hr.at[0], x_high), ix < dx - 1, ix > 0),
        (copy(xh_send.at[1], xh_recv.at[1], hs.at[1], hr.at[1], x_low), ix > 0, ix < dx - 1),
    ]
    pl.semaphore_wait(barrier, dx + dy - 2)
    for c, sends, takes in halos:
        pl.when(sends)(c.start)

    xm_copies = [
        copy(xm.at[ix], xm.at[ix], xms.at[o], xmr.at[o], {"gx": peer})
        for o, peer in enumerate(x_peers)
    ]
    for c in xm_copies:
        c.start()
    for p in range(planes):
        scr_d[p] = d[:, p].reshape(nx, ny).T
    dt = jnp.stack([scr_d[:, pl.ds(t, SUB, stride=ty), :] for t in range(ty)])
    yt, c, gl, gr = tree_matrix(dt, row_y)
    yrow, c, gl, gr = rows_matrix(c, gl, gr)
    put_matrix(
        ym, iy, c, gl, gr, [scr_d[p, 0:1, :] for p in range(planes)],
        [scr_d[p, ny - 1 : ny, :] for p in range(planes)],
    )
    ym_copies = [
        copy(ym.at[iy], ym.at[iy], yms.at[o], ymr.at[o], {"gy": peer})
        for o, peer in enumerate(y_peers)
    ]
    for c in ym_copies:
        c.start()

    source = []
    for cc in range(ncomp):
        for p in range(planes):
            f = cc * planes + p
            a = v[:, cc, p]
            lo = jnp.where(row == 0, 0.0, pltpu.roll(a[tx - 1], 1, 0))
            hi = jnp.where(row == SUB - 1, 0.0, pltpu.roll(a[0], SUB - 1, 0))
            grad_x = jnp.concatenate([a[1:], hi[None]], 0) - jnp.concatenate([lo[None], a[:-1]], 0)
            grad_y = jnp.where(lane == ny - 1, 0.0, pltpu.roll(fields[f], ny - 1, 1))
            grad_y = grad_y - jnp.where(lane == 0, 0.0, pltpu.roll(fields[f], 1, 1))
            grad_y = grad_y.reshape(tx, SUB, ny)
            source.append(a - scale * (v[:, 0, p] * grad_x + v[:, 1, p] * grad_y))
    side = jnp.where(lane == 0, scale, jnp.where(lane == ny - 1, -scale, 0.0))
    weight = [side * fields[planes + p] for p in range(planes)]

    for c in xm_copies:
        c.wait_recv()
    x_first, x_last, x_inner = ends_matrix(xm, dx, ix, planes, row)

    for c, sends, takes in halos:
        pl.when(takes)(c.wait_recv)
    take = lax.broadcasted_iota(jnp.int32, (2 * SUB, nx), 0) % 2 == 0
    halo = jnp.where(
        take,
        jnp.where(iy < dy - 1, pltpu.roll(yh_recv[1], 2 * SUB - 1, 0), 0.0),
        jnp.where(iy > 0, pltpu.roll(yh_recv[0], 1, 0), 0.0),
    )
    halo = jnp.where(lax.broadcasted_iota(jnp.int32, (2 * SUB, nx), 0) < 2 * nf, halo, 0.0)
    halo = jnp.concatenate([halo, jnp.zeros((ny - 2 * SUB, nx), jnp.float32)], 0).T
    for f in range(nf):
        near = pltpu.roll(halo, ny - 2 * f - 1, 1)
        source[f] = source[f] + (weight[f % planes] * near).reshape(tx, SUB, ny)
    source = jnp.stack(source, 1).reshape(v.shape)
    xmids, il, ir = tree_source(None, source, xt, wide)
    xrowmids, il, ir = rows_source(il, ir, xrow)
    own_first = pick(row % planes, [xh_send[1, p : p + 1, :] for p in range(planes)])
    own_last = pick(row % planes, [xh_send[0, p : p + 1, :] for p in range(planes)])
    il = tile_of(il, row) + scale * own_first * jnp.where(ix > 0, xh_recv[0], 0.0)
    ir = tile_of(ir, row) - scale * own_last * jnp.where(ix < dx - 1, xh_recv[1], 0.0)
    x_copies = [
        copy(xr_send.at[peer], xr_recv.at[ix], xs.at[o], xr.at[o], {"gx": peer})
        for o, peer in enumerate(x_peers)
    ]
    ends_send(xr_send, il, ir, x_first, x_last, x_copies)

    for c in ym_copies:
        c.wait_recv()
    y_first, y_last, y_inner = ends_matrix(ym, dy, iy, planes, row_y)

    for c in x_copies:
        c.wait_recv()
    low, high = ends_solve(xr_recv, il, ir, x_inner, dx, ix, ncomp, planes)
    left, right = rows_down(low, high, xrow, xrowmids, row)
    middle = tree_down(left, right, xt, xmids, wide)

    for f in range(nf):
        cc, p = f // planes, f % planes
        scr[cc, p] = middle[:, cc, p].reshape(nx, ny).T
    m = jnp.stack([scr[:, :, pl.ds(t, SUB, stride=ty), :] for t in range(ty)])
    ymids, il, ir = tree_source(None, m, yt, wide)
    yrowmids, il, ir = rows_source(il, ir, yrow)
    il, ir = tile_of(il, row_y), tile_of(ir, row_y)
    y_copies = [
        copy(yr_send.at[peer], yr_recv.at[iy], ys.at[o], yr.at[o], {"gy": peer})
        for o, peer in enumerate(y_peers)
    ]
    ends_send(yr_send, il, ir, y_first, y_last, y_copies)
    for c, sends, takes in halos:
        pl.when(sends)(c.wait_send)
    for c in xm_copies + ym_copies + x_copies + y_copies:
        c.wait_send()
    for c in y_copies:
        c.wait_recv()
    low, high = ends_solve(yr_recv, il, ir, y_inner, dy, iy, ncomp, planes)
    left, right = rows_down(low, high, yrow, yrowmids, row_y)
    w = tree_down(left, right, yt, ymids, wide)
    for t in range(ty):
        scr[:, :, pl.ds(t, SUB, stride=ty), :] = w[t]
    for f in range(nf):
        cc, p = f // planes, f % planes
        a = scr[cc, p].T.reshape(tx, SUB, ny)
        for t in range(tx):
            out[cc, p, pl.ds(t, SUB, stride=tx), :] = a[t]


def local(dx, dy, velocity, diffusion):
    ncomp, planes, nx, ny = velocity.shape
    vmem = pl.BlockSpec(memory_space=pltpu.VMEM)
    f32 = jnp.float32
    dma = pltpu.SemaphoreType.DMA
    return pl.pallas_call(
        functools.partial(kernel, dx, dy),
        out_shape=jax.ShapeDtypeStruct(velocity.shape, f32),
        in_specs=[pl.BlockSpec(memory_space=pl.ANY), vmem],
        out_specs=vmem,
        scratch_shapes=[
            pltpu.VMEM(velocity.shape, f32),
            pltpu.VMEM((2, SUB, ny), f32),
            pltpu.VMEM((2, SUB, ny), f32),
            pltpu.VMEM((2 * SUB, nx), f32),
            pltpu.VMEM((2, 2 * SUB, nx), f32),
            pltpu.VMEM((dx, 2 * SUB, ny), f32),
            pltpu.VMEM((dy, 2 * SUB, nx), f32),
            pltpu.VMEM((dx, SUB, ny), f32),
            pltpu.VMEM((dx, SUB, ny), f32),
            pltpu.VMEM((dy, SUB, nx), f32),
            pltpu.VMEM((dy, SUB, nx), f32),
            pltpu.VMEM((ncomp, planes, ny, nx), f32),
            pltpu.VMEM((planes, ny, nx), f32),
            dma((1,)), dma((4,)), dma((4,)),
            dma((dx,)), dma((dx,)), dma((dx,)), dma((dx,)),
            dma((dy,)), dma((dy,)), dma((dy,)), dma((dy,)),
        ],
        compiler_params=pltpu.CompilerParams(
            collective_id=0, has_side_effects=True, vmem_limit_bytes=54592 * 1024
        ),
    )(velocity, diffusion)


def solution(mesh):
    in_specs = (P(None, None, "gx", "gy"), P(None, "gx", "gy"))
    out_specs = P(None, None, "gx", "gy")
    body = functools.partial(local, mesh.shape["gx"], mesh.shape["gy"])
    return jax.shard_map(body, mesh=mesh, in_specs=in_specs, out_specs=out_specs, check_vma=False)
```

```python
import functools

import jax
import jax.numpy as jnp
from jax import lax
from jax.experimental import pallas as pl
from jax.experimental.pallas import tpu as pltpu
from jax.sharding import PartitionSpec as P

courant = 0.25
SUB = 8
MESH = pl.DeviceIdType.MESH


def halves(a):
    a = a.reshape((a.shape[0] // 2, 2) + a.shape[1:])
    return a[:, 0], a[:, 1]


def plus(a, b):
    return b if a is None else (a if b is None else a + b)


def join_matrix(c1, c2, gr1, gl2, gl1, gr2):
    g = gr1 + gl2
    r = 1.0 / (c1 + c2 + g)
    p, q = c1 * r, c2 * r
    return (p, q, r), p * c2, gl1 + p * g, gr2 + q * g


def tree_matrix(d, row):
    prev = jnp.concatenate([roll_rows(d[-1:], 1), d[:-1]], 0)
    c = 0.5 * (prev + d)
    kept = row == 0
    c1, c2 = halves(c)
    r = 1.0 / (c1 + c2 + 1.0)
    p, q = c1 * r, c2 * r
    p, q, r = (
        jnp.concatenate([jnp.where(kept, value, a[:1]), a[1:]], 0)
        for a, value in ((p, 1.0), (q, 0.0), (r, 0.0))
    )
    levels = [(p, q, r)]
    c, gl, gr = p * c2, p, 1.0 + q
    while c.shape[0] > 1:
        c1, c2 = halves(c)
        gr1, gr2 = halves(gr)
        gl1, gl2 = halves(gl)
        level, c, gl, gr = join_matrix(c1, c2, gr1, gl2, gl1, gr2)
        levels.append(level)
    return levels, c[0], gl[0], gr[0]


def tree_source(il, ir, levels, widen):
    mids = []
    for level in levels:
        p, q, r = (widen(a) for a in level)
        ir1, ir2 = halves(ir)
        il1, il2 = (None, None) if il is None else halves(il)
        i = plus(ir1, il2)
        mids.append(i * r)
        il = plus(il1, p * i)
        ir = ir2 + q * i
    return mids, il[0], ir[0]


def tree_down(left, right, levels, mids, widen):
    w = right[None]
    for level, mid in zip(reversed(levels), reversed(mids)):
        p, q = widen(level[0]), widen(level[1])
        wl = left[None] if w.shape[0] == 1 else jnp.concatenate([left[None], w[:-1]], 0)
        m = mid + p * wl + q * w
        w = jnp.stack([m, w], 1).reshape((2 * w.shape[0],) + w.shape[1:])
    return w


def roll_rows(a, shift):
    flat = a.reshape((-1,) + a.shape[-2:])
    out = [pltpu.roll(flat[k], shift % SUB, 0) for k in range(flat.shape[0])]
    return jnp.stack(out).reshape(a.shape)


def rows_matrix(c, gl, gr):
    levels = []
    for shift in (1, 2, 4):
        level, c, gl, gr = join_matrix(
            roll_rows(c, shift), c, roll_rows(gr, shift), gl, roll_rows(gl, shift), gr
        )
        levels.append(level)
    return levels, c, gl, gr


def rows_source(il, ir, levels):
    mids = []
    for shift, (p, q, r) in zip((1, 2, 4), levels):
        i = roll_rows(ir, shift) + il
        mids.append(i * r)
        il = roll_rows(il, shift) + p * i
        ir = ir + q * i
    return mids, il, ir


def rows_down(left, right, levels, mids, row):
    def solve(k, wl, wr):
        return mids[k] + levels[k][0] * wl + levels[k][1] * wr

    m = solve(2, left, right)
    m3 = jnp.broadcast_to(m[..., 7:8, :], m.shape)
    wr = jnp.where(row < 4, m3, right)
    m = solve(1, jnp.where(row < 4, left, m3), wr)
    m1 = jnp.broadcast_to(m[..., 3:4, :], m.shape)
    m5 = jnp.broadcast_to(m[..., 7:8, :], m.shape)
    wl = jnp.where(row < 2, left, jnp.where(row < 4, m1, jnp.where(row < 6, m3, m5)))
    wr = jnp.where(row < 2, m1, jnp.where(row < 4, m3, jnp.where(row < 6, m5, right)))
    m = solve(0, wl, wr)
    w = jnp.where(row % 2 == 1, wr, roll_rows(m, 7))
    return jnp.where(row == 0, left, roll_rows(w, 1)), w


def pick(place, items):
    out = items[0]
    for k in range(1, len(items)):
        out = jnp.where(place == k, items[k], out)
    return out


def tile_of(a, row):
    flat = a.reshape((-1,) + a.shape[-2:])
    out = jnp.zeros_like(flat[0])
    for f in range(flat.shape[0]):
        out = jnp.where(row == f, pltpu.roll(flat[f], (f + 1) % SUB, 0), out)
    return out


def put_matrix(ref, place, c, gl, gr, first, last):
    planes = c.shape[0]
    for p in range(planes):
        ref[place, p : p + 1, :] = c[p, SUB - 1 :]
        ref[place, planes + p : planes + p + 1, :] = gl[p, SUB - 1 :]
        ref[place, 2 * planes + p : 2 * planes + p + 1, :] = gr[p, SUB - 1 :]
        ref[place, 3 * planes + p : 3 * planes + p + 1, :] = first[p]
        ref[place, 4 * planes + p : 4 * planes + p + 1, :] = last[p]


def ends_matrix(ref, count, place, planes, row):
    def spread(k, quantity):
        return pick(
            row % planes,
            [ref[k, quantity * planes + p : quantity * planes + p + 1, :] for p in range(planes)],
        )

    c, gl, gr, first, last = ([spread(k, j) for k in range(count)] for j in range(5))
    link = [0.5 * (last[k - 1] + first[k]) if k else 0.5 * first[0] for k in range(count)]
    left, t_first, t_last = [gl[0] + link[0]], [], []
    right, u_first, u_last = [gr[-1] + 0.5 * last[-1]], [], []
    for k in range(count):
        t_first.append(c[k] / (c[k] + left[k]))
        g = gr[k] + t_first[k] * left[k]
        j = count - 1 - k
        u_last.insert(0, c[j] / (c[j] + right[0]))
        h = gl[j] + u_last[0] * right[0]
        if k < count - 1:
            t_last.append(link[k + 1] / (link[k + 1] + g))
            left.append(gl[k + 1] + t_last[k] * g)
            u_first.insert(0, link[j] / (link[j] + h))
            right.insert(0, gr[j - 1] + u_first[0] * h)
    u_first.insert(0, None)
    own_c, g, h = pick(place, c), pick(place, left), pick(place, right)
    r = 1.0 / (own_c * (g + h) + g * h)
    inner = ((own_c + h) * r, own_c * r, (own_c + g) * r)
    t_own, u_own = pick(place, t_first), pick(place, u_last)
    zero = jnp.zeros_like(own_c)
    from_first, from_last = [zero] * count, [zero] * count
    x = None
    for e in range(1, count):
        through = zero if x is None else x * t_first[e - 1] * t_last[e - 1]
        x = jnp.where(place == e - 1, t_last[e - 1], through)
        from_last[e], from_first[e] = x, x * t_own
    y = None
    for e in range(count - 2, -1, -1):
        through = zero if y is None else y * u_last[e + 1] * u_first[e + 1]
        y = jnp.where(place == e + 1, u_first[e + 1], through)
        from_first[e] = jnp.where(place > e, y, from_first[e])
        from_last[e] = jnp.where(place > e, y * u_own, from_last[e])
    return from_first, from_last, inner


def ends_send(send, il, ir, from_first, from_last, copies):
    for e in range(len(from_first)):
        send[e] = il * from_first[e] + ir * from_last[e]
    for c in copies:
        c.start()


def ends_solve(recv, il, ir, inner, count, place, ncomp, planes):
    for k in range(count):
        tile = recv[k]
        il = il + jnp.where(k < place, tile, 0.0)
        ir = ir + jnp.where(k > place, tile, 0.0)
    low = inner[0] * il + inner[1] * ir
    high = inner[1] * il + inner[2] * ir

    def split(a):
        parts = [jnp.broadcast_to(a[f : f + 1], a.shape) for f in range(ncomp * planes)]
        return jnp.stack(parts).reshape((ncomp, planes) + a.shape)

    return split(low), split(high)


def kernel(
    dx, dy, vel_in, dif_in, out,
    vel, dif, xh_send, xh_recv, yh_send, yh_recv,
    xm, ym, xr_send, xr_recv, yr_send, yr_recv, scr, scr_d,
    ins, hs, hr, xms, xmr, xs, xr, yms, ymr, ys, yr,
):
    ncomp, planes, nx, ny = vel.shape
    tx, ty = nx // SUB, ny // SUB
    nf = ncomp * planes
    ix, iy = lax.axis_index("gx"), lax.axis_index("gy")
    x_peers = [lax.rem(ix + o, dx) for o in range(1, dx)]
    y_peers = [lax.rem(iy + o, dy) for o in range(1, dy)]

    vel_copy = pltpu.make_async_copy(vel_in, vel, ins.at[0])
    dif_copy = pltpu.make_async_copy(dif_in, dif, ins.at[1])
    vel_copy.start()
    dif_copy.start()
    barrier = pltpu.get_barrier_semaphore()
    for peer in x_peers:
        pl.semaphore_signal(barrier, inc=1, device_id={"gx": peer}, device_id_type=MESH)
    for peer in y_peers:
        pl.semaphore_signal(barrier, inc=1, device_id={"gy": peer}, device_id_type=MESH)

    def copy(src, dst, send, recv, where):
        return pltpu.make_async_remote_copy(
            src_ref=src, dst_ref=dst, send_sem=send, recv_sem=recv,
            device_id=where, device_id_type=MESH,
        )

    def wide(a):
        return a[:, None]

    row = lax.broadcasted_iota(jnp.int32, (SUB, ny), 0)
    row_y = lax.broadcasted_iota(jnp.int32, (SUB, nx), 0)
    lane = lax.broadcasted_iota(jnp.int32, (nx, ny), 1)
    scale = 0.5 * courant

    vel_copy.wait()
    v = jnp.stack([vel[:, :, pl.ds(t, SUB, stride=tx), :] for t in range(tx)])
    fields = [v[:, c, p].reshape(nx, ny) for c in range(ncomp) for p in range(planes)]
    for f in range(nf):
        ref = vel.at[f // planes, f % planes]
        xh_send[0, f : f + 1, :] = ref[nx - 1 : nx, :]
        xh_send[1, f : f + 1, :] = ref[0:1, :]
    edges = jnp.zeros((nx, ny), jnp.float32)
    for f, a in enumerate(fields):
        edges = jnp.where(lane // 2 == f, pltpu.roll(a, 2 * f + 1, 1), edges)
    yh_send[...] = edges.T[: 2 * SUB]

    x_high, x_low = {"gx": lax.rem(ix + 1, dx)}, {"gx": lax.rem(ix + dx - 1, dx)}
    y_high, y_low = {"gy": lax.rem(iy + 1, dy)}, {"gy": lax.rem(iy + dy - 1, dy)}
    halos = [
        (copy(yh_send, yh_recv.at[0], hs.at[2], hr.at[2], y_high), iy < dy - 1, iy > 0),
        (copy(yh_send, yh_recv.at[1], hs.at[3], hr.at[3], y_low), iy > 0, iy < dy - 1),
        (copy(xh_send.at[0], xh_recv.at[0], hs.at[0], hr.at[0], x_high), ix < dx - 1, ix > 0),
        (copy(xh_send.at[1], xh_recv.at[1], hs.at[1], hr.at[1], x_low), ix > 0, ix < dx - 1),
    ]
    pl.semaphore_wait(barrier, dx + dy - 2)
    for c, sends, takes in halos:
        pl.when(sends)(c.start)

    dif_copy.wait()
    d = jnp.stack([dif[:, pl.ds(t, SUB, stride=tx), :] for t in range(tx)])
    xt, c, gl, gr = tree_matrix(d, row)
    xrow, c, gl, gr = rows_matrix(c, gl, gr)
    put_matrix(
        xm, ix, c, gl, gr, [dif[p, 0:1, :] for p in range(planes)],
        [dif[p, nx - 1 : nx, :] for p in range(planes)],
    )
    xm_copies = [
        copy(xm.at[ix], xm.at[ix], xms.at[o], xmr.at[o], {"gx": peer})
        for o, peer in enumerate(x_peers)
    ]
    for c in xm_copies:
        c.start()
    for p in range(planes):
        scr_d[p] = d[:, p].reshape(nx, ny).T
    dt = jnp.stack([scr_d[:, pl.ds(t, SUB, stride=ty), :] for t in range(ty)])
    yt, c, gl, gr = tree_matrix(dt, row_y)
    yrow, c, gl, gr = rows_matrix(c, gl, gr)
    put_matrix(
        ym, iy, c, gl, gr, [scr_d[p, 0:1, :] for p in range(planes)],
        [scr_d[p, ny - 1 : ny, :] for p in range(planes)],
    )
    ym_copies = [
        copy(ym.at[iy], ym.at[iy], yms.at[o], ymr.at[o], {"gy": peer})
        for o, peer in enumerate(y_peers)
    ]
    for c in ym_copies:
        c.start()

    source = []
    for cc in range(ncomp):
        for p in range(planes):
            f = cc * planes + p
            a = v[:, cc, p]
            lo = jnp.where(row == 0, 0.0, pltpu.roll(a[tx - 1], 1, 0))
            hi = jnp.where(row == SUB - 1, 0.0, pltpu.roll(a[0], SUB - 1, 0))
            grad_x = jnp.concatenate([a[1:], hi[None]], 0) - jnp.concatenate([lo[None], a[:-1]], 0)
            grad_y = jnp.where(lane == ny - 1, 0.0, pltpu.roll(fields[f], ny - 1, 1))
            grad_y = grad_y - jnp.where(lane == 0, 0.0, pltpu.roll(fields[f], 1, 1))
            grad_y = grad_y.reshape(tx, SUB, ny)
            source.append(a - scale * (v[:, 0, p] * grad_x + v[:, 1, p] * grad_y))
    side = jnp.where(lane == 0, scale, jnp.where(lane == ny - 1, -scale, 0.0))
    weight = [side * fields[planes + p] for p in range(planes)]

    for c in xm_copies:
        c.wait_recv()
    x_first, x_last, x_inner = ends_matrix(xm, dx, ix, planes, row)

    for c, sends, takes in halos:
        pl.when(takes)(c.wait_recv)
    take = lax.broadcasted_iota(jnp.int32, (2 * SUB, nx), 0) % 2 == 0
    halo = jnp.where(
        take,
        jnp.where(iy < dy - 1, pltpu.roll(yh_recv[1], 2 * SUB - 1, 0), 0.0),
        jnp.where(iy > 0, pltpu.roll(yh_recv[0], 1, 0), 0.0),
    )
    halo = jnp.where(lax.broadcasted_iota(jnp.int32, (2 * SUB, nx), 0) < 2 * nf, halo, 0.0)
    halo = jnp.concatenate([halo, jnp.zeros((ny - 2 * SUB, nx), jnp.float32)], 0).T
    for f in range(nf):
        near = pltpu.roll(halo, ny - 2 * f - 1, 1)
        source[f] = source[f] + (weight[f % planes] * near).reshape(tx, SUB, ny)
    source = jnp.stack(source, 1).reshape(v.shape)
    xmids, il, ir = tree_source(None, source, xt, wide)
    xrowmids, il, ir = rows_source(il, ir, xrow)
    own_first = pick(row % planes, [xh_send[1, p : p + 1, :] for p in range(planes)])
    own_last = pick(row % planes, [xh_send[0, p : p + 1, :] for p in range(planes)])
    il = tile_of(il, row) + scale * own_first * jnp.where(ix > 0, xh_recv[0], 0.0)
    ir = tile_of(ir, row) - scale * own_last * jnp.where(ix < dx - 1, xh_recv[1], 0.0)
    x_copies = [
        copy(xr_send.at[peer], xr_recv.at[ix], xs.at[o], xr.at[o], {"gx": peer})
        for o, peer in enumerate(x_peers)
    ]
    ends_send(xr_send, il, ir, x_first, x_last, x_copies)

    for c in ym_copies:
        c.wait_recv()
    y_first, y_last, y_inner = ends_matrix(ym, dy, iy, planes, row_y)

    for c in x_copies:
        c.wait_recv()
    low, high = ends_solve(xr_recv, il, ir, x_inner, dx, ix, ncomp, planes)
    left, right = rows_down(low, high, xrow, xrowmids, row)
    middle = tree_down(left, right, xt, xmids, wide)

    for f in range(nf):
        cc, p = f // planes, f % planes
        scr[cc, p] = middle[:, cc, p].reshape(nx, ny).T
    m = jnp.stack([scr[:, :, pl.ds(t, SUB, stride=ty), :] for t in range(ty)])
    ymids, il, ir = tree_source(None, m, yt, wide)
    yrowmids, il, ir = rows_source(il, ir, yrow)
    il, ir = tile_of(il, row_y), tile_of(ir, row_y)
    y_copies = [
        copy(yr_send.at[peer], yr_recv.at[iy], ys.at[o], yr.at[o], {"gy": peer})
        for o, peer in enumerate(y_peers)
    ]
    ends_send(yr_send, il, ir, y_first, y_last, y_copies)
    for c, sends, takes in halos:
        pl.when(sends)(c.wait_send)
    for c in xm_copies + ym_copies + x_copies + y_copies:
        c.wait_send()
    for c in y_copies:
        c.wait_recv()
    low, high = ends_solve(yr_recv, il, ir, y_inner, dy, iy, ncomp, planes)
    left, right = rows_down(low, high, yrow, yrowmids, row_y)
    w = tree_down(left, right, yt, ymids, wide)
    for t in range(ty):
        scr[:, :, pl.ds(t, SUB, stride=ty), :] = w[t]
    for f in range(nf):
        cc, p = f // planes, f % planes
        a = scr[cc, p].T.reshape(tx, SUB, ny)
        for t in range(tx):
            out[cc, p, pl.ds(t, SUB, stride=tx), :] = a[t]


def local(dx, dy, velocity, diffusion):
    ncomp, planes, nx, ny = velocity.shape
    vmem = pl.BlockSpec(memory_space=pltpu.VMEM)
    f32 = jnp.float32
    dma = pltpu.SemaphoreType.DMA
    return pl.pallas_call(
        functools.partial(kernel, dx, dy),
        out_shape=pltpu.VMEM(velocity.shape, f32),
        in_specs=[pl.BlockSpec(memory_space=pltpu.HBM)] * 2,
        out_specs=vmem,
        scratch_shapes=[
            pltpu.VMEM(velocity.shape, f32),
            pltpu.VMEM(diffusion.shape, f32),
            pltpu.VMEM((2, SUB, ny), f32),
            pltpu.VMEM((2, SUB, ny), f32),
            pltpu.VMEM((2 * SUB, nx), f32),
            pltpu.VMEM((2, 2 * SUB, nx), f32),
            pltpu.VMEM((dx, 2 * SUB, ny), f32),
            pltpu.VMEM((dy, 2 * SUB, nx), f32),
            pltpu.VMEM((dx, SUB, ny), f32),
            pltpu.VMEM((dx, SUB, ny), f32),
            pltpu.VMEM((dy, SUB, nx), f32),
            pltpu.VMEM((dy, SUB, nx), f32),
            pltpu.VMEM((ncomp, planes, ny, nx), f32),
            pltpu.VMEM((planes, ny, nx), f32),
            dma((2,)), dma((4,)), dma((4,)),
            dma((dx,)), dma((dx,)), dma((dx,)), dma((dx,)),
            dma((dy,)), dma((dy,)), dma((dy,)), dma((dy,)),
        ],
        compiler_params=pltpu.CompilerParams(
            collective_id=0, has_side_effects=True, vmem_limit_bytes=32 * 1024 * 1024
        ),
    )(
        pltpu.with_memory_space_constraint(velocity, pltpu.HBM),
        pltpu.with_memory_space_constraint(diffusion, pltpu.HBM),
    )


def solution(mesh):
    in_specs = (P(None, None, "gx", "gy"), P(None, "gx", "gy"))
    out_specs = P(None, None, "gx", "gy")
    body = functools.partial(local, mesh.shape["gx"], mesh.shape["gy"])
    return jax.shard_map(body, mesh=mesh, in_specs=in_specs, out_specs=out_specs, check_vma=False)
```

```python
import functools

import jax
import jax.numpy as jnp
from jax import lax
from jax.experimental import pallas as pl
from jax.experimental.pallas import tpu as pltpu
from jax.sharding import PartitionSpec as P

courant = 0.25
SUB = 8
MESH = pl.DeviceIdType.MESH


def halves(a):
    a = a.reshape((a.shape[0] // 2, 2) + a.shape[1:])
    return a[:, 0], a[:, 1]


def plus(a, b):
    return b if a is None else (a if b is None else a + b)


def join_matrix(c1, c2, gr1, gl2, gl1, gr2):
    g = gr1 + gl2
    r = 1.0 / (c1 + c2 + g)
    p, q = c1 * r, c2 * r
    return (p, q, r), p * c2, gl1 + p * g, gr2 + q * g


def tree_matrix(d, row):
    prev = jnp.concatenate([roll_rows(d[-1:], 1), d[:-1]], 0)
    c = 0.5 * (prev + d)
    kept = row == 0
    c1, c2 = halves(c)
    r = 1.0 / (c1 + c2 + 1.0)
    p, q = c1 * r, c2 * r
    p, q, r = (
        jnp.concatenate([jnp.where(kept, value, a[:1]), a[1:]], 0)
        for a, value in ((p, 1.0), (q, 0.0), (r, 0.0))
    )
    levels = [(p, q, r)]
    c, gl, gr = p * c2, p, 1.0 + q
    while c.shape[0] > 1:
        c1, c2 = halves(c)
        gr1, gr2 = halves(gr)
        gl1, gl2 = halves(gl)
        level, c, gl, gr = join_matrix(c1, c2, gr1, gl2, gl1, gr2)
        levels.append(level)
    return levels, c[0], gl[0], gr[0]


def tree_source(il, ir, levels, widen):
    mids = []
    for level in levels:
        p, q, r = (widen(a) for a in level)
        ir1, ir2 = halves(ir)
        il1, il2 = (None, None) if il is None else halves(il)
        i = plus(ir1, il2)
        mids.append(i * r)
        il = plus(il1, p * i)
        ir = ir2 + q * i
    return mids, il[0], ir[0]


def tree_down(left, right, levels, mids, widen):
    w = right[None]
    for level, mid in zip(reversed(levels), reversed(mids)):
        p, q = widen(level[0]), widen(level[1])
        wl = left[None] if w.shape[0] == 1 else jnp.concatenate([left[None], w[:-1]], 0)
        m = mid + p * wl + q * w
        w = jnp.stack([m, w], 1).reshape((2 * w.shape[0],) + w.shape[1:])
    return w


def roll_rows(a, shift):
    flat = a.reshape((-1,) + a.shape[-2:])
    out = [pltpu.roll(flat[k], shift % SUB, 0) for k in range(flat.shape[0])]
    return jnp.stack(out).reshape(a.shape)


def rows_matrix(c, gl, gr):
    levels = []
    for shift in (1, 2, 4):
        level, c, gl, gr = join_matrix(
            roll_rows(c, shift), c, roll_rows(gr, shift), gl, roll_rows(gl, shift), gr
        )
        levels.append(level)
    return levels, c, gl, gr


def rows_source(il, ir, levels):
    mids = []
    for shift, (p, q, r) in zip((1, 2, 4), levels):
        i = roll_rows(ir, shift) + il
        mids.append(i * r)
        il = roll_rows(il, shift) + p * i
        ir = ir + q * i
    return mids, il, ir


def rows_down(left, right, levels, mids, row):
    def solve(k, wl, wr):
        return mids[k] + levels[k][0] * wl + levels[k][1] * wr

    m = solve(2, left, right)
    m3 = jnp.broadcast_to(m[..., 7:8, :], m.shape)
    wr = jnp.where(row < 4, m3, right)
    m = solve(1, jnp.where(row < 4, left, m3), wr)
    m1 = jnp.broadcast_to(m[..., 3:4, :], m.shape)
    m5 = jnp.broadcast_to(m[..., 7:8, :], m.shape)
    wl = jnp.where(row < 2, left, jnp.where(row < 4, m1, jnp.where(row < 6, m3, m5)))
    wr = jnp.where(row < 2, m1, jnp.where(row < 4, m3, jnp.where(row < 6, m5, right)))
    m = solve(0, wl, wr)
    w = jnp.where(row % 2 == 1, wr, roll_rows(m, 7))
    return jnp.where(row == 0, left, roll_rows(w, 1)), w


def end_shapes(levels, row_levels, row):
    one = jnp.ones_like(row_levels[0][0])
    out = []
    for left, right in ((one, 0.0 * one), (0.0 * one, one)):
        low, high = rows_down(left, right, row_levels, [0.0] * 3, row)
        out.append(tree_down(low, high, levels, [0.0] * len(levels), lambda a: a))
    return out


def inner_part(source, levels, row_levels, row, widen):
    mids, il, ir = tree_source(None, source, levels, widen)
    row_mids, il, ir = rows_source(il, ir, row_levels)
    zero = jnp.zeros_like(il)
    low, high = rows_down(zero, zero, row_levels, row_mids, row)
    return tree_down(low, high, levels, mids, widen)


def pick(place, items):
    out = items[0]
    for k in range(1, len(items)):
        out = jnp.where(place == k, items[k], out)
    return out


def tile_of(a, row):
    flat = a.reshape((-1,) + a.shape[-2:])
    out = jnp.zeros_like(flat[0])
    for f in range(flat.shape[0]):
        out = jnp.where(row == f, jnp.sum(flat[f], axis=0, keepdims=True), out)
    return out


def put_matrix(ref, place, c, gl, gr, first, last):
    planes = c.shape[0]
    for p in range(planes):
        ref[place, p : p + 1, :] = c[p, SUB - 1 :]
        ref[place, planes + p : planes + p + 1, :] = gl[p, SUB - 1 :]
        ref[place, 2 * planes + p : 2 * planes + p + 1, :] = gr[p, SUB - 1 :]
        ref[place, 3 * planes + p : 3 * planes + p + 1, :] = first[p]
        ref[place, 4 * planes + p : 4 * planes + p + 1, :] = last[p]


def ends_matrix(ref, count, place, planes, row):
    def spread(k, quantity):
        return pick(
            row % planes,
            [ref[k, quantity * planes + p : quantity * planes + p + 1, :] for p in range(planes)],
        )

    c, gl, gr, first, last = ([spread(k, j) for k in range(count)] for j in range(5))
    link = [0.5 * (last[k - 1] + first[k]) if k else 0.5 * first[0] for k in range(count)]
    left, t_first, t_last = [gl[0] + link[0]], [], []
    right, u_first, u_last = [gr[-1] + 0.5 * last[-1]], [], []
    for k in range(count):
        t_first.append(c[k] / (c[k] + left[k]))
        g = gr[k] + t_first[k] * left[k]
        j = count - 1 - k
        u_last.insert(0, c[j] / (c[j] + right[0]))
        h = gl[j] + u_last[0] * right[0]
        if k < count - 1:
            t_last.append(link[k + 1] / (link[k + 1] + g))
            left.append(gl[k + 1] + t_last[k] * g)
            u_first.insert(0, link[j] / (link[j] + h))
            right.insert(0, gr[j - 1] + u_first[0] * h)
    u_first.insert(0, None)
    own_c, g, h = pick(place, c), pick(place, left), pick(place, right)
    r = 1.0 / (own_c * (g + h) + g * h)
    inner = ((own_c + h) * r, own_c * r, (own_c + g) * r)
    t_own, u_own = pick(place, t_first), pick(place, u_last)
    zero = jnp.zeros_like(own_c)
    from_first, from_last = [zero] * count, [zero] * count
    x = None
    for e in range(1, count):
        through = zero if x is None else x * t_first[e - 1] * t_last[e - 1]
        x = jnp.where(place == e - 1, t_last[e - 1], through)
        from_last[e], from_first[e] = x, x * t_own
    y = None
    for e in range(count - 2, -1, -1):
        through = zero if y is None else y * u_last[e + 1] * u_first[e + 1]
        y = jnp.where(place == e + 1, u_first[e + 1], through)
        from_first[e] = jnp.where(place > e, y, from_first[e])
        from_last[e] = jnp.where(place > e, y * u_own, from_last[e])
    return from_first, from_last, inner


def ends_send(send, il, ir, from_first, from_last, copies):
    for e in range(len(from_first)):
        send[e] = il * from_first[e] + ir * from_last[e]
    for c in copies:
        c.start()


def ends_solve(recv, il, ir, inner, count, place):
    for k in range(count):
        tile = recv[k]
        il = il + jnp.where(k < place, tile, 0.0)
        ir = ir + jnp.where(k > place, tile, 0.0)
    low = inner[0] * il + inner[1] * ir
    high = inner[1] * il + inner[2] * ir

    return low, high


def kernel(
    dx, dy, vel_in, dif_in, out,
    vel, dif, xh_send, xh_recv, yh_send, yh_recv,
    xm, ym, xr_send, xr_recv, yr_send, yr_recv, scr, scr_d,
    ins, hs, hr, xms, xmr, xs, xr, yms, ymr, ys, yr,
):
    ncomp, planes, nx, ny = vel.shape
    tx, ty = nx // SUB, ny // SUB
    nf = ncomp * planes
    ix, iy = lax.axis_index("gx"), lax.axis_index("gy")
    x_peers = [lax.rem(ix + o, dx) for o in range(1, dx)]
    y_peers = [lax.rem(iy + o, dy) for o in range(1, dy)]

    vel_copy = pltpu.make_async_copy(vel_in, vel, ins.at[0])
    dif_copy = pltpu.make_async_copy(dif_in, dif, ins.at[1])
    vel_copy.start()
    dif_copy.start()
    barrier = pltpu.get_barrier_semaphore()
    for peer in x_peers:
        pl.semaphore_signal(barrier, inc=1, device_id={"gx": peer}, device_id_type=MESH)
    for peer in y_peers:
        pl.semaphore_signal(barrier, inc=1, device_id={"gy": peer}, device_id_type=MESH)

    def copy(src, dst, send, recv, where):
        return pltpu.make_async_remote_copy(
            src_ref=src, dst_ref=dst, send_sem=send, recv_sem=recv,
            device_id=where, device_id_type=MESH,
        )

    def wide(a):
        return a[:, None]

    row = lax.broadcasted_iota(jnp.int32, (SUB, ny), 0)
    row_y = lax.broadcasted_iota(jnp.int32, (SUB, nx), 0)
    lane = lax.broadcasted_iota(jnp.int32, (nx, ny), 1)
    scale = 0.5 * courant

    vel_copy.wait()
    v = jnp.stack([vel[:, :, pl.ds(t, SUB, stride=tx), :] for t in range(tx)])
    fields = [v[:, c, p].reshape(nx, ny) for c in range(ncomp) for p in range(planes)]
    for f in range(nf):
        ref = vel.at[f // planes, f % planes]
        xh_send[0, f : f + 1, :] = ref[nx - 1 : nx, :]
        xh_send[1, f : f + 1, :] = ref[0:1, :]
    edges = jnp.zeros((nx, ny), jnp.float32)
    for f, a in enumerate(fields):
        edges = jnp.where(lane // 2 == f, pltpu.roll(a, 2 * f + 1, 1), edges)
    yh_send[...] = edges.T[: 2 * SUB]

    x_high, x_low = {"gx": lax.rem(ix + 1, dx)}, {"gx": lax.rem(ix + dx - 1, dx)}
    y_high, y_low = {"gy": lax.rem(iy + 1, dy)}, {"gy": lax.rem(iy + dy - 1, dy)}
    halos = [
        (copy(yh_send, yh_recv.at[0], hs.at[2], hr.at[2], y_high), iy < dy - 1, iy > 0),
        (copy(yh_send, yh_recv.at[1], hs.at[3], hr.at[3], y_low), iy > 0, iy < dy - 1),
        (copy(xh_send.at[0], xh_recv.at[0], hs.at[0], hr.at[0], x_high), ix < dx - 1, ix > 0),
        (copy(xh_send.at[1], xh_recv.at[1], hs.at[1], hr.at[1], x_low), ix > 0, ix < dx - 1),
    ]
    pl.semaphore_wait(barrier, dx + dy - 2)
    for c, sends, takes in halos:
        pl.when(sends)(c.start)

    dif_copy.wait()
    d = jnp.stack([dif[:, pl.ds(t, SUB, stride=tx), :] for t in range(tx)])
    xt, c, gl, gr = tree_matrix(d, row)
    xrow, c, gl, gr = rows_matrix(c, gl, gr)
    put_matrix(
        xm, ix, c, gl, gr, [dif[p, 0:1, :] for p in range(planes)],
        [dif[p, nx - 1 : nx, :] for p in range(planes)],
    )
    xm_copies = [
        copy(xm.at[ix], xm.at[ix], xms.at[o], xmr.at[o], {"gx": peer})
        for o, peer in enumerate(x_peers)
    ]
    for c in xm_copies:
        c.start()
    for p in range(planes):
        scr_d[p] = d[:, p].reshape(nx, ny).T
    dt = jnp.stack([scr_d[:, pl.ds(t, SUB, stride=ty), :] for t in range(ty)])
    yt, c, gl, gr = tree_matrix(dt, row_y)
    yrow, c, gl, gr = rows_matrix(c, gl, gr)
    put_matrix(
        ym, iy, c, gl, gr, [scr_d[p, 0:1, :] for p in range(planes)],
        [scr_d[p, ny - 1 : ny, :] for p in range(planes)],
    )
    ym_copies = [
        copy(ym.at[iy], ym.at[iy], yms.at[o], ymr.at[o], {"gy": peer})
        for o, peer in enumerate(y_peers)
    ]
    for c in ym_copies:
        c.start()

    source = []
    for cc in range(ncomp):
        for p in range(planes):
            f = cc * planes + p
            a = v[:, cc, p]
            lo = jnp.where(row == 0, 0.0, pltpu.roll(a[tx - 1], 1, 0))
            hi = jnp.where(row == SUB - 1, 0.0, pltpu.roll(a[0], SUB - 1, 0))
            grad_x = jnp.concatenate([a[1:], hi[None]], 0) - jnp.concatenate([lo[None], a[:-1]], 0)
            grad_y = jnp.where(lane == ny - 1, 0.0, pltpu.roll(fields[f], ny - 1, 1))
            grad_y = grad_y - jnp.where(lane == 0, 0.0, pltpu.roll(fields[f], 1, 1))
            grad_y = grad_y.reshape(tx, SUB, ny)
            source.append(a - scale * (v[:, 0, p] * grad_x + v[:, 1, p] * grad_y))
    side = jnp.where(lane == 0, scale, jnp.where(lane == ny - 1, -scale, 0.0))
    weight = [side * fields[planes + p] for p in range(planes)]

    x_left, x_right = end_shapes(xt, xrow, row)
    for c in xm_copies:
        c.wait_recv()
    x_first, x_last, x_inner = ends_matrix(xm, dx, ix, planes, row)

    for c, sends, takes in halos:
        pl.when(takes)(c.wait_recv)
    take = lax.broadcasted_iota(jnp.int32, (2 * SUB, nx), 0) % 2 == 0
    halo = jnp.where(
        take,
        jnp.where(iy < dy - 1, pltpu.roll(yh_recv[1], 2 * SUB - 1, 0), 0.0),
        jnp.where(iy > 0, pltpu.roll(yh_recv[0], 1, 0), 0.0),
    )
    halo = jnp.where(lax.broadcasted_iota(jnp.int32, (2 * SUB, nx), 0) < 2 * nf, halo, 0.0)
    halo = jnp.concatenate([halo, jnp.zeros((ny - 2 * SUB, nx), jnp.float32)], 0).T
    for f in range(nf):
        near = pltpu.roll(halo, ny - 2 * f - 1, 1)
        source[f] = source[f] + (weight[f % planes] * near).reshape(tx, SUB, ny)
    source = jnp.stack(source, 1).reshape(v.shape)
    own_first = pick(row % planes, [xh_send[1, p : p + 1, :] for p in range(planes)])
    own_last = pick(row % planes, [xh_send[0, p : p + 1, :] for p in range(planes)])
    il = tile_of(jnp.sum(wide(x_left) * source, axis=0), row) + scale * own_first * jnp.where(ix > 0, xh_recv[0], 0.0)
    ir = tile_of(jnp.sum(wide(x_right) * source, axis=0), row) - scale * own_last * jnp.where(ix < dx - 1, xh_recv[1], 0.0)
    x_copies = [
        copy(xr_send.at[peer], xr_recv.at[ix], xs.at[o], xr.at[o], {"gx": peer})
        for o, peer in enumerate(x_peers)
    ]
    ends_send(xr_send, il, ir, x_first, x_last, x_copies)

    for c in ym_copies:
        c.wait_recv()
    y_first, y_last, y_inner = ends_matrix(ym, dy, iy, planes, row_y)

    middle = inner_part(source, xt, xrow, row, wide)
    shapes = []
    for shape in end_shapes(yt, yrow, row_y):
        for t in range(ty):
            scr_d[:, pl.ds(t, SUB, stride=ty), :] = shape[t]
        shapes.append([scr_d[p].T for p in range(planes)])
    y_left, y_right = shapes

    for c in x_copies:
        c.wait_recv()
    low, high = ends_solve(xr_recv, il, ir, x_inner, dx, ix)
    middle = [
        middle[:, f // planes, f % planes]
        + x_left[:, f % planes] * low[f : f + 1]
        + x_right[:, f % planes] * high[f : f + 1]
        for f in range(nf)
    ]
    middle = [a.reshape(nx, ny) for a in middle]
    ends = jnp.zeros((nx, ny), jnp.float32)
    for f, a in enumerate(middle):
        at_left = jnp.sum(a * y_left[f % planes], axis=1, keepdims=True)
        at_right = jnp.sum(a * y_right[f % planes], axis=1, keepdims=True)
        ends = jnp.where(lane == f, at_left, jnp.where(lane == SUB + f, at_right, ends))
    ends = ends.T
    il, ir = ends[:SUB], ends[SUB : 2 * SUB]
    y_copies = [
        copy(yr_send.at[peer], yr_recv.at[iy], ys.at[o], yr.at[o], {"gy": peer})
        for o, peer in enumerate(y_peers)
    ]
    ends_send(yr_send, il, ir, y_first, y_last, y_copies)

    for f in range(nf):
        scr[f // planes, f % planes] = middle[f].T
    m = jnp.stack([scr[:, :, pl.ds(t, SUB, stride=ty), :] for t in range(ty)])
    w = inner_part(m, yt, yrow, row_y, wide)
    for t in range(ty):
        scr[:, :, pl.ds(t, SUB, stride=ty), :] = w[t]
    w = [scr[f // planes, f % planes].T for f in range(nf)]
    for c, sends, takes in halos:
        pl.when(sends)(c.wait_send)
    for c in xm_copies + ym_copies + x_copies + y_copies:
        c.wait_send()

    for c in y_copies:
        c.wait_recv()
    low, high = ends_solve(yr_recv, il, ir, y_inner, dy, iy)
    blank = jnp.zeros((ny - 2 * SUB, nx), jnp.float32)
    ends = jnp.concatenate([low, high, blank], 0).T
    for f in range(nf):
        p = f % planes
        a = w[f] + y_left[p] * ends[:, f : f + 1] + y_right[p] * ends[:, SUB + f : SUB + f + 1]
        a = a.reshape(tx, SUB, ny)
        for t in range(tx):
            out[f // planes, p, pl.ds(t, SUB, stride=tx), :] = a[t]


def local(dx, dy, velocity, diffusion):
    ncomp, planes, nx, ny = velocity.shape
    vmem = pl.BlockSpec(memory_space=pltpu.VMEM)
    f32 = jnp.float32
    dma = pltpu.SemaphoreType.DMA
    return pl.pallas_call(
        functools.partial(kernel, dx, dy),
        out_shape=pltpu.VMEM(velocity.shape, f32),
        in_specs=[pl.BlockSpec(memory_space=pltpu.HBM)] * 2,
        out_specs=vmem,
        scratch_shapes=[
            pltpu.VMEM(velocity.shape, f32),
            pltpu.VMEM(diffusion.shape, f32),
            pltpu.VMEM((2, SUB, ny), f32),
            pltpu.VMEM((2, SUB, ny), f32),
            pltpu.VMEM((2 * SUB, nx), f32),
            pltpu.VMEM((2, 2 * SUB, nx), f32),
            pltpu.VMEM((dx, 2 * SUB, ny), f32),
            pltpu.VMEM((dy, 2 * SUB, nx), f32),
            pltpu.VMEM((dx, SUB, ny), f32),
            pltpu.VMEM((dx, SUB, ny), f32),
            pltpu.VMEM((dy, SUB, nx), f32),
            pltpu.VMEM((dy, SUB, nx), f32),
            pltpu.VMEM((ncomp, planes, ny, nx), f32),
            pltpu.VMEM((planes, ny, nx), f32),
            dma((2,)), dma((4,)), dma((4,)),
            dma((dx,)), dma((dx,)), dma((dx,)), dma((dx,)),
            dma((dy,)), dma((dy,)), dma((dy,)), dma((dy,)),
        ],
        compiler_params=pltpu.CompilerParams(
            collective_id=0, has_side_effects=True, vmem_limit_bytes=32 * 1024 * 1024
        ),
    )(
        pltpu.with_memory_space_constraint(velocity, pltpu.HBM),
        pltpu.with_memory_space_constraint(diffusion, pltpu.HBM),
    )


def solution(mesh):
    in_specs = (P(None, None, "gx", "gy"), P(None, "gx", "gy"))
    out_specs = P(None, None, "gx", "gy")
    body = functools.partial(local, mesh.shape["gx"], mesh.shape["gy"])
    return jax.shard_map(body, mesh=mesh, in_specs=in_specs, out_specs=out_specs, check_vma=False)
```

```python
import functools

import jax
import jax.numpy as jnp
from jax import lax
from jax.experimental import pallas as pl
from jax.experimental.pallas import tpu as pltpu
from jax.sharding import PartitionSpec as P

courant = 0.25
SUB = 8
MESH = pl.DeviceIdType.MESH


def halves(a):
    a = a.reshape((a.shape[0] // 2, 2) + a.shape[1:])
    return a[:, 0], a[:, 1]


def plus(a, b):
    return b if a is None else (a if b is None else a + b)


def join_matrix(c1, c2, gr1, gl2, gl1, gr2):
    g = gr1 + gl2
    r = 1.0 / (c1 + c2 + g)
    p, q = c1 * r, c2 * r
    return (p, q, r), p * c2, gl1 + p * g, gr2 + q * g


def tree_matrix(d, row):
    prev = jnp.concatenate([roll_rows(d[-1:], 1), d[:-1]], 0)
    c = 0.5 * (prev + d)
    kept = row == 0
    c1, c2 = halves(c)
    r = 1.0 / (c1 + c2 + 1.0)
    p, q = c1 * r, c2 * r
    p, q, r = (
        jnp.concatenate([jnp.where(kept, value, a[:1]), a[1:]], 0)
        for a, value in ((p, 1.0), (q, 0.0), (r, 0.0))
    )
    levels = [(p, q, r)]
    c, gl, gr = p * c2, p, 1.0 + q
    while c.shape[0] > 1:
        c1, c2 = halves(c)
        gr1, gr2 = halves(gr)
        gl1, gl2 = halves(gl)
        level, c, gl, gr = join_matrix(c1, c2, gr1, gl2, gl1, gr2)
        levels.append(level)
    return levels, c[0], gl[0], gr[0]


def tree_source(il, ir, levels, widen):
    mids = []
    for level in levels:
        p, q, r = (widen(a) for a in level)
        ir1, ir2 = halves(ir)
        il1, il2 = (None, None) if il is None else halves(il)
        i = plus(ir1, il2)
        mids.append(i * r)
        il = plus(il1, p * i)
        ir = ir2 + q * i
    return mids, il[0], ir[0]


def tree_down(left, right, levels, mids, widen):
    w = right[None]
    for level, mid in zip(reversed(levels), reversed(mids)):
        p, q = widen(level[0]), widen(level[1])
        wl = left[None] if w.shape[0] == 1 else jnp.concatenate([left[None], w[:-1]], 0)
        m = mid + p * wl + q * w
        w = jnp.stack([m, w], 1).reshape((2 * w.shape[0],) + w.shape[1:])
    return w


def roll_rows(a, shift):
    flat = a.reshape((-1,) + a.shape[-2:])
    out = [pltpu.roll(flat[k], shift % SUB, 0) for k in range(flat.shape[0])]
    return jnp.stack(out).reshape(a.shape)


def rows_matrix(c, gl, gr):
    levels = []
    for shift in (1, 2, 4):
        level, c, gl, gr = join_matrix(
            roll_rows(c, shift), c, roll_rows(gr, shift), gl, roll_rows(gl, shift), gr
        )
        levels.append(level)
    return levels, c, gl, gr


def rows_source(il, ir, levels):
    mids = []
    for shift, (p, q, r) in zip((1, 2, 4), levels):
        i = roll_rows(ir, shift) + il
        mids.append(i * r)
        il = roll_rows(il, shift) + p * i
        ir = ir + q * i
    return mids, il, ir


def rows_down(left, right, levels, mids, row):
    def solve(k, wl, wr):
        return mids[k] + levels[k][0] * wl + levels[k][1] * wr

    m = solve(2, left, right)
    m3 = jnp.broadcast_to(m[..., 7:8, :], m.shape)
    wr = jnp.where(row < 4, m3, right)
    m = solve(1, jnp.where(row < 4, left, m3), wr)
    m1 = jnp.broadcast_to(m[..., 3:4, :], m.shape)
    m5 = jnp.broadcast_to(m[..., 7:8, :], m.shape)
    wl = jnp.where(row < 2, left, jnp.where(row < 4, m1, jnp.where(row < 6, m3, m5)))
    wr = jnp.where(row < 2, m1, jnp.where(row < 4, m3, jnp.where(row < 6, m5, right)))
    m = solve(0, wl, wr)
    w = jnp.where(row % 2 == 1, wr, roll_rows(m, 7))
    return jnp.where(row == 0, left, roll_rows(w, 1)), w


def end_shapes(levels, row_levels, row):
    one = jnp.ones_like(row_levels[0][0])
    out = []
    for left, right in ((one, 0.0 * one), (0.0 * one, one)):
        low, high = rows_down(left, right, row_levels, [0.0] * 3, row)
        out.append(tree_down(low, high, levels, [0.0] * len(levels), lambda a: a))
    return out


def inner_part(source, levels, row_levels, row, widen):
    mids, il, ir = tree_source(None, source, levels, widen)
    row_mids, il, ir = rows_source(il, ir, row_levels)
    zero = jnp.zeros_like(il)
    low, high = rows_down(zero, zero, row_levels, row_mids, row)
    return tree_down(low, high, levels, mids, widen)


def pick(place, items):
    out = items[0]
    for k in range(1, len(items)):
        out = jnp.where(place == k, items[k], out)
    return out


def put_matrix(ref, place, c, gl, gr, first, last):
    planes = c.shape[0]
    for p in range(planes):
        ref[place, p : p + 1, :] = c[p, SUB - 1 :]
        ref[place, planes + p : planes + p + 1, :] = gl[p, SUB - 1 :]
        ref[place, 2 * planes + p : 2 * planes + p + 1, :] = gr[p, SUB - 1 :]
        ref[place, 3 * planes + p : 3 * planes + p + 1, :] = first[p]
        ref[place, 4 * planes + p : 4 * planes + p + 1, :] = last[p]


def ends_matrix(ref, count, place, planes, row):
    def spread(k, quantity):
        return pick(
            row % planes,
            [ref[k, quantity * planes + p : quantity * planes + p + 1, :] for p in range(planes)],
        )

    c, gl, gr, first, last = ([spread(k, j) for k in range(count)] for j in range(5))
    link = [0.5 * (last[k - 1] + first[k]) if k else 0.5 * first[0] for k in range(count)]
    left, t_first, t_last = [gl[0] + link[0]], [], []
    right, u_first, u_last = [gr[-1] + 0.5 * last[-1]], [], []
    for k in range(count):
        t_first.append(c[k] / (c[k] + left[k]))
        g = gr[k] + t_first[k] * left[k]
        j = count - 1 - k
        u_last.insert(0, c[j] / (c[j] + right[0]))
        h = gl[j] + u_last[0] * right[0]
        if k < count - 1:
            t_last.append(link[k + 1] / (link[k + 1] + g))
            left.append(gl[k + 1] + t_last[k] * g)
            u_first.insert(0, link[j] / (link[j] + h))
            right.insert(0, gr[j - 1] + u_first[0] * h)
    u_first.insert(0, None)
    own_c, g, h = pick(place, c), pick(place, left), pick(place, right)
    r = 1.0 / (own_c * (g + h) + g * h)
    inner = ((own_c + h) * r, own_c * r, (own_c + g) * r)
    t_own, u_own = pick(place, t_first), pick(place, u_last)
    zero = jnp.zeros_like(own_c)
    from_first, from_last = [zero] * count, [zero] * count
    x = None
    for e in range(1, count):
        through = zero if x is None else x * t_first[e - 1] * t_last[e - 1]
        x = jnp.where(place == e - 1, t_last[e - 1], through)
        from_last[e], from_first[e] = x, x * t_own
    y = None
    for e in range(count - 2, -1, -1):
        through = zero if y is None else y * u_last[e + 1] * u_first[e + 1]
        y = jnp.where(place == e + 1, u_first[e + 1], through)
        from_first[e] = jnp.where(place > e, y, from_first[e])
        from_last[e] = jnp.where(place > e, y * u_own, from_last[e])
    return from_first, from_last, inner


def ends_send(send, il, ir, from_first, from_last, copies):
    for e in range(len(from_first)):
        send[e] = il * from_first[e] + ir * from_last[e]
    for c in copies:
        c.start()


def ends_solve(recv, il, ir, inner, count, place):
    for k in range(count):
        tile = recv[k]
        il = il + jnp.where(k < place, tile, 0.0)
        ir = ir + jnp.where(k > place, tile, 0.0)
    low = inner[0] * il + inner[1] * ir
    high = inner[1] * il + inner[2] * ir

    return low, high


def kernel(
    dx, dy, vel_in, dif_in, out,
    vel, dif, xh_send, xh_recv, yh_send, yh_recv,
    xm, ym, xr_send, xr_recv, yr_send, yr_recv, scr, scr_d, v, src, ends_x,
    ins, hs, hr, xms, xmr, xs, xr, yms, ymr, ys, yr,
):
    ncomp, planes, nx, ny = vel.shape
    tx, ty = nx // SUB, ny // SUB
    nf = ncomp * planes
    ix, iy = lax.axis_index("gx"), lax.axis_index("gy")
    x_peers = [lax.rem(ix + o, dx) for o in range(1, dx)]
    y_peers = [lax.rem(iy + o, dy) for o in range(1, dy)]

    vel_copy = pltpu.make_async_copy(vel_in, vel, ins.at[0])
    dif_copy = pltpu.make_async_copy(dif_in, dif, ins.at[1])
    vel_copy.start()
    dif_copy.start()
    barrier = pltpu.get_barrier_semaphore()
    for peer in x_peers:
        pl.semaphore_signal(barrier, inc=1, device_id={"gx": peer}, device_id_type=MESH)
    for peer in y_peers:
        pl.semaphore_signal(barrier, inc=1, device_id={"gy": peer}, device_id_type=MESH)

    def copy(src, dst, send, recv, where):
        return pltpu.make_async_remote_copy(
            src_ref=src, dst_ref=dst, send_sem=send, recv_sem=recv,
            device_id=where, device_id_type=MESH,
        )

    def same(a):
        return a

    row = lax.broadcasted_iota(jnp.int32, (SUB, ny), 0)
    row_y = lax.broadcasted_iota(jnp.int32, (SUB, nx), 0)
    lane = lax.broadcasted_iota(jnp.int32, (nx, ny), 1)
    scale = 0.5 * courant

    vel_copy.wait()
    for t in range(tx):
        v[t] = vel[:, :, pl.ds(t, SUB, stride=tx), :]

    def field(c, p):
        return v[:, c, p].reshape(nx, ny)

    for f in range(nf):
        ref = vel.at[f // planes, f % planes]
        xh_send[0, f : f + 1, :] = ref[nx - 1 : nx, :]
        xh_send[1, f : f + 1, :] = ref[0:1, :]
    def add_edges(k, edges):
        c = ncomp - 1 - k
        for p in range(planes - 1, -1, -1):
            edges = jnp.where(lane < 2, pltpu.roll(field(c, p), 1, 1), pltpu.roll(edges, 2, 1))
        return edges

    edges = lax.fori_loop(0, ncomp, add_edges, jnp.zeros((nx, ny), jnp.float32))
    yh_send[...] = edges.T[: 2 * SUB]

    x_high, x_low = {"gx": lax.rem(ix + 1, dx)}, {"gx": lax.rem(ix + dx - 1, dx)}
    y_high, y_low = {"gy": lax.rem(iy + 1, dy)}, {"gy": lax.rem(iy + dy - 1, dy)}
    halos = [
        (copy(yh_send, yh_recv.at[0], hs.at[2], hr.at[2], y_high), iy < dy - 1, iy > 0),
        (copy(yh_send, yh_recv.at[1], hs.at[3], hr.at[3], y_low), iy > 0, iy < dy - 1),
        (copy(xh_send.at[0], xh_recv.at[0], hs.at[0], hr.at[0], x_high), ix < dx - 1, ix > 0),
        (copy(xh_send.at[1], xh_recv.at[1], hs.at[1], hr.at[1], x_low), ix > 0, ix < dx - 1),
    ]
    pl.semaphore_wait(barrier, dx + dy - 2)
    for c, sends, takes in halos:
        pl.when(sends)(c.start)

    dif_copy.wait()
    d = jnp.stack([dif[:, pl.ds(t, SUB, stride=tx), :] for t in range(tx)])
    xt, c, gl, gr = tree_matrix(d, row)
    xrow, c, gl, gr = rows_matrix(c, gl, gr)
    put_matrix(
        xm, ix, c, gl, gr, [dif[p, 0:1, :] for p in range(planes)],
        [dif[p, nx - 1 : nx, :] for p in range(planes)],
    )
    xm_copies = [
        copy(xm.at[ix], xm.at[ix], xms.at[o], xmr.at[o], {"gx": peer})
        for o, peer in enumerate(x_peers)
    ]
    for c in xm_copies:
        c.start()
    for p in range(planes):
        scr_d[p] = d[:, p].reshape(nx, ny).T
    dt = jnp.stack([scr_d[:, pl.ds(t, SUB, stride=ty), :] for t in range(ty)])
    yt, c, gl, gr = tree_matrix(dt, row_y)
    yrow, c, gl, gr = rows_matrix(c, gl, gr)
    put_matrix(
        ym, iy, c, gl, gr, [scr_d[p, 0:1, :] for p in range(planes)],
        [scr_d[p, ny - 1 : ny, :] for p in range(planes)],
    )
    ym_copies = [
        copy(ym.at[iy], ym.at[iy], yms.at[o], ymr.at[o], {"gy": peer})
        for o, peer in enumerate(y_peers)
    ]
    for c in ym_copies:
        c.start()

    @pl.loop(0, ncomp)
    def _(c):
        for p in range(planes):
            a = v[:, c, p]
            flat = field(c, p)
            lo = jnp.where(row == 0, 0.0, pltpu.roll(a[tx - 1], 1, 0))
            hi = jnp.where(row == SUB - 1, 0.0, pltpu.roll(a[0], SUB - 1, 0))
            grad_x = jnp.concatenate([a[1:], hi[None]], 0) - jnp.concatenate([lo[None], a[:-1]], 0)
            grad_y = jnp.where(lane == ny - 1, 0.0, pltpu.roll(flat, ny - 1, 1))
            grad_y = grad_y - jnp.where(lane == 0, 0.0, pltpu.roll(flat, 1, 1))
            grad_y = grad_y.reshape(tx, SUB, ny)
            src[c, :, p] = a - scale * (v[:, 0, p] * grad_x + v[:, 1, p] * grad_y)

    side = jnp.where(lane == 0, scale, jnp.where(lane == ny - 1, -scale, 0.0))

    x_left, x_right = end_shapes(xt, xrow, row)
    for c in xm_copies:
        c.wait_recv()
    x_first, x_last, x_inner = ends_matrix(xm, dx, ix, planes, row)

    for c, sends, takes in halos:
        pl.when(takes)(c.wait_recv)
    take = lax.broadcasted_iota(jnp.int32, (2 * SUB, nx), 0) % 2 == 0
    halo = jnp.where(
        take,
        jnp.where(iy < dy - 1, pltpu.roll(yh_recv[1], 2 * SUB - 1, 0), 0.0),
        jnp.where(iy > 0, pltpu.roll(yh_recv[0], 1, 0), 0.0),
    )
    halo = jnp.where(lax.broadcasted_iota(jnp.int32, (2 * SUB, nx), 0) < 2 * nf, halo, 0.0)
    halo = jnp.concatenate([halo, jnp.zeros((ny - 2 * SUB, nx), jnp.float32)], 0).T

    def add_halo(c, state):
        near, il, ir = state
        for p in range(planes):
            f = c * planes + p
            a = src[c, :, p] + (side * field(1, p) * near).reshape(tx, SUB, ny)
            src[c, :, p] = a
            at_left = jnp.sum(jnp.sum(x_left[:, p] * a, axis=0), axis=0, keepdims=True)
            at_right = jnp.sum(jnp.sum(x_right[:, p] * a, axis=0), axis=0, keepdims=True)
            il, ir = jnp.where(row == f, at_left, il), jnp.where(row == f, at_right, ir)
            near = pltpu.roll(near, ny - 2, 1)
        return near, il, ir

    blank = jnp.zeros((SUB, ny), jnp.float32)
    _, il, ir = lax.fori_loop(0, ncomp, add_halo, (pltpu.roll(halo, ny - 1, 1), blank, blank))
    own_first = pick(row % planes, [xh_send[1, p : p + 1, :] for p in range(planes)])
    own_last = pick(row % planes, [xh_send[0, p : p + 1, :] for p in range(planes)])
    il = il + scale * own_first * jnp.where(ix > 0, xh_recv[0], 0.0)
    ir = ir - scale * own_last * jnp.where(ix < dx - 1, xh_recv[1], 0.0)
    x_copies = [
        copy(xr_send.at[peer], xr_recv.at[ix], xs.at[o], xr.at[o], {"gx": peer})
        for o, peer in enumerate(x_peers)
    ]
    ends_send(xr_send, il, ir, x_first, x_last, x_copies)

    for c in ym_copies:
        c.wait_recv()
    y_first, y_last, y_inner = ends_matrix(ym, dy, iy, planes, row_y)

    @pl.loop(0, ncomp)
    def _(c):
        src[c] = inner_part(src[c], xt, xrow, row, same)

    shapes = []
    for shape in end_shapes(yt, yrow, row_y):
        for t in range(ty):
            scr_d[:, pl.ds(t, SUB, stride=ty), :] = shape[t]
        shapes.append([scr_d[p].T for p in range(planes)])
    y_left, y_right = shapes

    for c in x_copies:
        c.wait_recv()
    low, high = ends_solve(xr_recv, il, ir, x_inner, dx, ix)
    ends_x[0], ends_x[1] = low, high

    def add_ends(k, ends):
        c = ncomp - 1 - k
        for p in range(planes - 1, -1, -1):
            f = c * planes + p
            a = src[c, :, p] + x_left[:, p] * ends_x[0, pl.ds(f, 1), :]
            a = a + x_right[:, p] * ends_x[1, pl.ds(f, 1), :]
            src[c, :, p] = a
            a = a.reshape(nx, ny)
            at_left = jnp.sum(a * y_left[p], axis=1, keepdims=True)
            at_right = jnp.sum(a * y_right[p], axis=1, keepdims=True)
            ends = pltpu.roll(ends, 1, 1)
            ends = jnp.where(lane == 0, at_left, jnp.where(lane == SUB, at_right, ends))
        return ends

    ends = lax.fori_loop(0, ncomp, add_ends, jnp.zeros((nx, ny), jnp.float32)).T
    il, ir = ends[:SUB], ends[SUB : 2 * SUB]
    y_copies = [
        copy(yr_send.at[peer], yr_recv.at[iy], ys.at[o], yr.at[o], {"gy": peer})
        for o, peer in enumerate(y_peers)
    ]
    ends_send(yr_send, il, ir, y_first, y_last, y_copies)

    @pl.loop(0, ncomp)
    def _(c):
        for p in range(planes):
            scr[c, p] = src[c, :, p].reshape(nx, ny).T
        m = jnp.stack([scr[c, :, pl.ds(t, SUB, stride=ty), :] for t in range(ty)])
        w = inner_part(m, yt, yrow, row_y, same)
        for t in range(ty):
            scr[c, :, pl.ds(t, SUB, stride=ty), :] = w[t]
        for p in range(planes):
            src[c, :, p] = scr[c, p].T.reshape(tx, SUB, ny)

    for c, sends, takes in halos:
        pl.when(sends)(c.wait_send)
    for c in xm_copies + ym_copies + x_copies + y_copies:
        c.wait_send()

    for c in y_copies:
        c.wait_recv()
    low, high = ends_solve(yr_recv, il, ir, y_inner, dy, iy)
    blank = jnp.zeros((ny - 2 * SUB, nx), jnp.float32)
    ends = jnp.concatenate([low, high, blank], 0).T

    def finish(c, ends):
        for p in range(planes):
            a = y_left[p] * ends[:, 0:1] + y_right[p] * ends[:, SUB : SUB + 1]
            a = src[c, :, p] + a.reshape(tx, SUB, ny)
            for t in range(tx):
                out[c, p, pl.ds(t, SUB, stride=tx), :] = a[t]
            ends = pltpu.roll(ends, ny - 1, 1)
        return ends

    lax.fori_loop(0, ncomp, finish, ends)


def local(dx, dy, velocity, diffusion):
    ncomp, planes, nx, ny = velocity.shape
    vmem = pl.BlockSpec(memory_space=pltpu.VMEM)
    f32 = jnp.float32
    dma = pltpu.SemaphoreType.DMA
    return pl.pallas_call(
        functools.partial(kernel, dx, dy),
        out_shape=pltpu.VMEM(velocity.shape, f32),
        in_specs=[pl.BlockSpec(memory_space=pltpu.HBM)] * 2,
        out_specs=vmem,
        scratch_shapes=[
            pltpu.VMEM(velocity.shape, f32),
            pltpu.VMEM(diffusion.shape, f32),
            pltpu.VMEM((2, SUB, ny), f32),
            pltpu.VMEM((2, SUB, ny), f32),
            pltpu.VMEM((2 * SUB, nx), f32),
            pltpu.VMEM((2, 2 * SUB, nx), f32),
            pltpu.VMEM((dx, 2 * SUB, ny), f32),
            pltpu.VMEM((dy, 2 * SUB, nx), f32),
            pltpu.VMEM((dx, SUB, ny), f32),
            pltpu.VMEM((dx, SUB, ny), f32),
            pltpu.VMEM((dy, SUB, nx), f32),
            pltpu.VMEM((dy, SUB, nx), f32),
            pltpu.VMEM((ncomp, planes, ny, nx), f32),
            pltpu.VMEM((planes, ny, nx), f32),
            pltpu.VMEM((nx // SUB, ncomp, planes, SUB, ny), f32),
            pltpu.VMEM((ncomp, nx // SUB, planes, SUB, ny), f32),
            pltpu.VMEM((2, SUB, ny), f32),
            dma((2,)), dma((4,)), dma((4,)),
            dma((dx,)), dma((dx,)), dma((dx,)), dma((dx,)),
            dma((dy,)), dma((dy,)), dma((dy,)), dma((dy,)),
        ],
        compiler_params=pltpu.CompilerParams(
            collective_id=0, has_side_effects=True, vmem_limit_bytes=32 * 1024 * 1024
        ),
    )(
        pltpu.with_memory_space_constraint(velocity, pltpu.HBM),
        pltpu.with_memory_space_constraint(diffusion, pltpu.HBM),
    )


def solution(mesh):
    in_specs = (P(None, None, "gx", "gy"), P(None, "gx", "gy"))
    out_specs = P(None, None, "gx", "gy")
    body = functools.partial(local, mesh.shape["gx"], mesh.shape["gy"])
    return jax.shard_map(body, mesh=mesh, in_specs=in_specs, out_specs=out_specs, check_vma=False)
```

```python
import functools

import jax
import jax.numpy as jnp
from jax import lax
from jax.experimental import pallas as pl
from jax.experimental.pallas import tpu as pltpu
from jax.sharding import PartitionSpec as P

courant = 0.25
SUB = 8
MESH = pl.DeviceIdType.MESH


def halves(a):
    a = a.reshape((a.shape[0] // 2, 2) + a.shape[1:])
    return a[:, 0], a[:, 1]


def plus(a, b):
    return b if a is None else (a if b is None else a + b)


def join_matrix(c1, c2, gr1, gl2, gl1, gr2):
    g = gr1 + gl2
    r = 1.0 / (c1 + c2 + g)
    p, q = c1 * r, c2 * r
    return (p, q, r), p * c2, gl1 + p * g, gr2 + q * g


def tree_matrix(d, row):
    prev = jnp.concatenate([roll_rows(d[-1:], 1), d[:-1]], 0)
    c = 0.5 * (prev + d)
    kept = row == 0
    c1, c2 = halves(c)
    r = 1.0 / (c1 + c2 + 1.0)
    p, q = c1 * r, c2 * r
    p, q, r = (
        jnp.concatenate([jnp.where(kept, value, a[:1]), a[1:]], 0)
        for a, value in ((p, 1.0), (q, 0.0), (r, 0.0))
    )
    levels = [(p, q, r)]
    c, gl, gr = p * c2, p, 1.0 + q
    while c.shape[0] > 1:
        c1, c2 = halves(c)
        gr1, gr2 = halves(gr)
        gl1, gl2 = halves(gl)
        level, c, gl, gr = join_matrix(c1, c2, gr1, gl2, gl1, gr2)
        levels.append(level)
    return levels, c[0], gl[0], gr[0]


def tree_source(il, ir, levels, widen):
    mids = []
    for level in levels:
        p, q, r = (widen(a) for a in level)
        ir1, ir2 = halves(ir)
        il1, il2 = (None, None) if il is None else halves(il)
        i = plus(ir1, il2)
        mids.append(i * r)
        il = plus(il1, p * i)
        ir = ir2 + q * i
    return mids, il[0], ir[0]


def tree_down(left, right, levels, mids, widen):
    w = right[None]
    for level, mid in zip(reversed(levels), reversed(mids)):
        p, q = widen(level[0]), widen(level[1])
        wl = left[None] if w.shape[0] == 1 else jnp.concatenate([left[None], w[:-1]], 0)
        m = mid + p * wl + q * w
        w = jnp.stack([m, w], 1).reshape((2 * w.shape[0],) + w.shape[1:])
    return w


def roll_rows(a, shift):
    flat = a.reshape((-1,) + a.shape[-2:])
    out = [pltpu.roll(flat[k], shift % SUB, 0) for k in range(flat.shape[0])]
    return jnp.stack(out).reshape(a.shape)


def rows_matrix(c, gl, gr):
    levels = []
    for shift in (1, 2, 4):
        level, c, gl, gr = join_matrix(
            roll_rows(c, shift), c, roll_rows(gr, shift), gl, roll_rows(gl, shift), gr
        )
        levels.append(level)
    return levels, c, gl, gr


def rows_source(il, ir, levels):
    mids = []
    for shift, (p, q, r) in zip((1, 2, 4), levels):
        i = roll_rows(ir, shift) + il
        mids.append(i * r)
        il = roll_rows(il, shift) + p * i
        ir = ir + q * i
    return mids, il, ir


def rows_down(left, right, levels, mids, row):
    def solve(k, wl, wr):
        return mids[k] + levels[k][0] * wl + levels[k][1] * wr

    m = solve(2, left, right)
    m3 = jnp.broadcast_to(m[..., 7:8, :], m.shape)
    wr = jnp.where(row < 4, m3, right)
    m = solve(1, jnp.where(row < 4, left, m3), wr)
    m1 = jnp.broadcast_to(m[..., 3:4, :], m.shape)
    m5 = jnp.broadcast_to(m[..., 7:8, :], m.shape)
    wl = jnp.where(row < 2, left, jnp.where(row < 4, m1, jnp.where(row < 6, m3, m5)))
    wr = jnp.where(row < 2, m1, jnp.where(row < 4, m3, jnp.where(row < 6, m5, right)))
    m = solve(0, wl, wr)
    w = jnp.where(row % 2 == 1, wr, roll_rows(m, 7))
    return jnp.where(row == 0, left, roll_rows(w, 1)), w


def end_shapes(levels, row_levels, row):
    one = jnp.ones_like(row_levels[0][0])
    out = []
    for left, right in ((one, 0.0 * one), (0.0 * one, one)):
        low, high = rows_down(left, right, row_levels, [0.0] * 3, row)
        out.append(tree_down(low, high, levels, [0.0] * len(levels), lambda a: a))
    return out


def pick(place, items):
    out = items[0]
    for k in range(1, len(items)):
        out = jnp.where(place == k, items[k], out)
    return out


def tile_of(a, row):
    flat = a.reshape((-1,) + a.shape[-2:])
    out = jnp.zeros_like(flat[0])
    for f in range(flat.shape[0]):
        out = jnp.where(row == f, pltpu.roll(flat[f], (f + 1) % SUB, 0), out)
    return out


def put_matrix(ref, place, c, gl, gr, first, last):
    planes = c.shape[0]
    for p in range(planes):
        ref[place, p : p + 1, :] = c[p, SUB - 1 :]
        ref[place, planes + p : planes + p + 1, :] = gl[p, SUB - 1 :]
        ref[place, 2 * planes + p : 2 * planes + p + 1, :] = gr[p, SUB - 1 :]
        ref[place, 3 * planes + p : 3 * planes + p + 1, :] = first[p]
        ref[place, 4 * planes + p : 4 * planes + p + 1, :] = last[p]


def ends_matrix(ref, count, place, planes, row):
    def spread(k, quantity):
        return pick(
            row % planes,
            [ref[k, quantity * planes + p : quantity * planes + p + 1, :] for p in range(planes)],
        )

    c, gl, gr, first, last = ([spread(k, j) for k in range(count)] for j in range(5))
    link = [0.5 * (last[k - 1] + first[k]) if k else 0.5 * first[0] for k in range(count)]
    left, t_first, t_last = [gl[0] + link[0]], [], []
    right, u_first, u_last = [gr[-1] + 0.5 * last[-1]], [], []
    for k in range(count):
        t_first.append(c[k] / (c[k] + left[k]))
        g = gr[k] + t_first[k] * left[k]
        j = count - 1 - k
        u_last.insert(0, c[j] / (c[j] + right[0]))
        h = gl[j] + u_last[0] * right[0]
        if k < count - 1:
            t_last.append(link[k + 1] / (link[k + 1] + g))
            left.append(gl[k + 1] + t_last[k] * g)
            u_first.insert(0, link[j] / (link[j] + h))
            right.insert(0, gr[j - 1] + u_first[0] * h)
    u_first.insert(0, None)
    own_c, g, h = pick(place, c), pick(place, left), pick(place, right)
    r = 1.0 / (own_c * (g + h) + g * h)
    inner = ((own_c + h) * r, own_c * r, (own_c + g) * r)
    t_own, u_own = pick(place, t_first), pick(place, u_last)
    zero = jnp.zeros_like(own_c)
    from_first, from_last = [zero] * count, [zero] * count
    x = None
    for e in range(1, count):
        through = zero if x is None else x * t_first[e - 1] * t_last[e - 1]
        x = jnp.where(place == e - 1, t_last[e - 1], through)
        from_last[e], from_first[e] = x, x * t_own
    y = None
    for e in range(count - 2, -1, -1):
        through = zero if y is None else y * u_last[e + 1] * u_first[e + 1]
        y = jnp.where(place == e + 1, u_first[e + 1], through)
        from_first[e] = jnp.where(place > e, y, from_first[e])
        from_last[e] = jnp.where(place > e, y * u_own, from_last[e])
    return from_first, from_last, inner


def ends_send(send, il, ir, from_first, from_last, copies):
    for e in range(len(from_first)):
        send[e] = il * from_first[e] + ir * from_last[e]
    for c in copies:
        c.start()


def ends_solve(recv, il, ir, inner, count, place):
    for k in range(count):
        tile = recv[k]
        il = il + jnp.where(k < place, tile, 0.0)
        ir = ir + jnp.where(k > place, tile, 0.0)
    low = inner[0] * il + inner[1] * ir
    high = inner[1] * il + inner[2] * ir

    return low, high


def kernel(
    dx, dy, vel_in, dif_in, out,
    vel, dif, xh_send, xh_recv, yh_send, yh_recv,
    xm, ym, xr_send, xr_recv, yr_send, yr_recv, scr, scr_d,
    ins, hs, hr, xms, xmr, xs, xr, yms, ymr, ys, yr,
):
    ncomp, planes, nx, ny = vel.shape
    tx, ty = nx // SUB, ny // SUB
    nf = ncomp * planes
    ix, iy = lax.axis_index("gx"), lax.axis_index("gy")
    x_peers = [lax.rem(ix + o, dx) for o in range(1, dx)]
    y_peers = [lax.rem(iy + o, dy) for o in range(1, dy)]

    vel_copy = pltpu.make_async_copy(vel_in, vel, ins.at[0])
    dif_copy = pltpu.make_async_copy(dif_in, dif, ins.at[1])
    vel_copy.start()
    dif_copy.start()
    barrier = pltpu.get_barrier_semaphore()
    for peer in x_peers:
        pl.semaphore_signal(barrier, inc=1, device_id={"gx": peer}, device_id_type=MESH)
    for peer in y_peers:
        pl.semaphore_signal(barrier, inc=1, device_id={"gy": peer}, device_id_type=MESH)

    def copy(src, dst, send, recv, where):
        return pltpu.make_async_remote_copy(
            src_ref=src, dst_ref=dst, send_sem=send, recv_sem=recv,
            device_id=where, device_id_type=MESH,
        )

    def wide(a):
        return a[:, None]

    row = lax.broadcasted_iota(jnp.int32, (SUB, ny), 0)
    row_y = lax.broadcasted_iota(jnp.int32, (SUB, nx), 0)
    lane = lax.broadcasted_iota(jnp.int32, (nx, ny), 1)
    scale = 0.5 * courant

    vel_copy.wait()
    v = jnp.stack([vel[:, :, pl.ds(t, SUB, stride=tx), :] for t in range(tx)])
    fields = [v[:, c, p].reshape(nx, ny) for c in range(ncomp) for p in range(planes)]
    for f in range(nf):
        ref = vel.at[f // planes, f % planes]
        xh_send[0, f : f + 1, :] = ref[nx - 1 : nx, :]
        xh_send[1, f : f + 1, :] = ref[0:1, :]
    edges = jnp.zeros((nx, ny), jnp.float32)
    for f, a in enumerate(fields):
        edges = jnp.where(lane // 2 == f, pltpu.roll(a, 2 * f + 1, 1), edges)
    yh_send[...] = edges.T[: 2 * SUB]

    x_high, x_low = {"gx": lax.rem(ix + 1, dx)}, {"gx": lax.rem(ix + dx - 1, dx)}
    y_high, y_low = {"gy": lax.rem(iy + 1, dy)}, {"gy": lax.rem(iy + dy - 1, dy)}
    halos = [
        (copy(yh_send, yh_recv.at[0], hs.at[2], hr.at[2], y_high), iy < dy - 1, iy > 0),
        (copy(yh_send, yh_recv.at[1], hs.at[3], hr.at[3], y_low), iy > 0, iy < dy - 1),
        (copy(xh_send.at[0], xh_recv.at[0], hs.at[0], hr.at[0], x_high), ix < dx - 1, ix > 0),
        (copy(xh_send.at[1], xh_recv.at[1], hs.at[1], hr.at[1], x_low), ix > 0, ix < dx - 1),
    ]
    pl.semaphore_wait(barrier, dx + dy - 2)
    for c, sends, takes in halos:
        pl.when(sends)(c.start)

    dif_copy.wait()
    d = jnp.stack([dif[:, pl.ds(t, SUB, stride=tx), :] for t in range(tx)])
    xt, c, gl, gr = tree_matrix(d, row)
    xrow, c, gl, gr = rows_matrix(c, gl, gr)
    put_matrix(
        xm, ix, c, gl, gr, [dif[p, 0:1, :] for p in range(planes)],
        [dif[p, nx - 1 : nx, :] for p in range(planes)],
    )
    xm_copies = [
        copy(xm.at[ix], xm.at[ix], xms.at[o], xmr.at[o], {"gx": peer})
        for o, peer in enumerate(x_peers)
    ]
    for c in xm_copies:
        c.start()
    for p in range(planes):
        scr_d[p] = d[:, p].reshape(nx, ny).T
    dt = jnp.stack([scr_d[:, pl.ds(t, SUB, stride=ty), :] for t in range(ty)])
    yt, c, gl, gr = tree_matrix(dt, row_y)
    yrow, c, gl, gr = rows_matrix(c, gl, gr)
    put_matrix(
        ym, iy, c, gl, gr, [scr_d[p, 0:1, :] for p in range(planes)],
        [scr_d[p, ny - 1 : ny, :] for p in range(planes)],
    )
    ym_copies = [
        copy(ym.at[iy], ym.at[iy], yms.at[o], ymr.at[o], {"gy": peer})
        for o, peer in enumerate(y_peers)
    ]
    for c in ym_copies:
        c.start()

    source = []
    for cc in range(ncomp):
        for p in range(planes):
            f = cc * planes + p
            a = v[:, cc, p]
            lo = jnp.where(row == 0, 0.0, pltpu.roll(a[tx - 1], 1, 0))
            hi = jnp.where(row == SUB - 1, 0.0, pltpu.roll(a[0], SUB - 1, 0))
            grad_x = jnp.concatenate([a[1:], hi[None]], 0) - jnp.concatenate([lo[None], a[:-1]], 0)
            grad_y = jnp.where(lane == ny - 1, 0.0, pltpu.roll(fields[f], ny - 1, 1))
            grad_y = grad_y - jnp.where(lane == 0, 0.0, pltpu.roll(fields[f], 1, 1))
            grad_y = grad_y.reshape(tx, SUB, ny)
            source.append(a - scale * (v[:, 0, p] * grad_x + v[:, 1, p] * grad_y))
    side = jnp.where(lane == 0, scale, jnp.where(lane == ny - 1, -scale, 0.0))
    weight = [side * fields[planes + p] for p in range(planes)]

    for c in xm_copies:
        c.wait_recv()
    x_first, x_last, x_inner = ends_matrix(xm, dx, ix, planes, row)

    for c, sends, takes in halos:
        pl.when(takes)(c.wait_recv)
    take = lax.broadcasted_iota(jnp.int32, (2 * SUB, nx), 0) % 2 == 0
    halo = jnp.where(
        take,
        jnp.where(iy < dy - 1, pltpu.roll(yh_recv[1], 2 * SUB - 1, 0), 0.0),
        jnp.where(iy > 0, pltpu.roll(yh_recv[0], 1, 0), 0.0),
    )
    halo = jnp.where(lax.broadcasted_iota(jnp.int32, (2 * SUB, nx), 0) < 2 * nf, halo, 0.0)
    halo = jnp.concatenate([halo, jnp.zeros((ny - 2 * SUB, nx), jnp.float32)], 0).T
    for f in range(nf):
        near = pltpu.roll(halo, ny - 2 * f - 1, 1)
        source[f] = source[f] + (weight[f % planes] * near).reshape(tx, SUB, ny)
    source = jnp.stack(source, 1).reshape(v.shape)
    xmids, il, ir = tree_source(None, source, xt, wide)
    xrowmids, il, ir = rows_source(il, ir, xrow)
    own_first = pick(row % planes, [xh_send[1, p : p + 1, :] for p in range(planes)])
    own_last = pick(row % planes, [xh_send[0, p : p + 1, :] for p in range(planes)])
    il = tile_of(il, row) + scale * own_first * jnp.where(ix > 0, xh_recv[0], 0.0)
    ir = tile_of(ir, row) - scale * own_last * jnp.where(ix < dx - 1, xh_recv[1], 0.0)
    x_copies = [
        copy(xr_send.at[peer], xr_recv.at[ix], xs.at[o], xr.at[o], {"gx": peer})
        for o, peer in enumerate(x_peers)
    ]
    ends_send(xr_send, il, ir, x_first, x_last, x_copies)

    for c in ym_copies:
        c.wait_recv()
    y_first, y_last, y_inner = ends_matrix(ym, dy, iy, planes, row_y)

    shapes = []
    for shape in end_shapes(yt, yrow, row_y):
        for t in range(ty):
            scr_d[:, pl.ds(t, SUB, stride=ty), :] = shape[t]
        shapes.append([scr_d[p].T for p in range(planes)])
    y_left, y_right = shapes

    def split(a):
        parts = [jnp.broadcast_to(a[f : f + 1], a.shape) for f in range(nf)]
        return jnp.stack(parts).reshape((ncomp, planes) + a.shape)

    for c in x_copies:
        c.wait_recv()
    low, high = (split(a) for a in ends_solve(xr_recv, il, ir, x_inner, dx, ix))
    left, right = rows_down(low, high, xrow, xrowmids, row)
    middle = tree_down(left, right, xt, xmids, wide)

    for f in range(nf):
        cc, p = f // planes, f % planes
        scr[cc, p] = middle[:, cc, p].reshape(nx, ny).T
    m = jnp.stack([scr[:, :, pl.ds(t, SUB, stride=ty), :] for t in range(ty)])
    ymids, il, ir = tree_source(None, m, yt, wide)
    yrowmids, il, ir = rows_source(il, ir, yrow)
    il, ir = tile_of(il, row_y), tile_of(ir, row_y)
    y_copies = [
        copy(yr_send.at[peer], yr_recv.at[iy], ys.at[o], yr.at[o], {"gy": peer})
        for o, peer in enumerate(y_peers)
    ]
    ends_send(yr_send, il, ir, y_first, y_last, y_copies)

    zero = jnp.zeros_like(m[0])
    left, right = rows_down(zero, zero, yrow, yrowmids, row_y)
    w = tree_down(left, right, yt, ymids, wide)
    for t in range(ty):
        scr[:, :, pl.ds(t, SUB, stride=ty), :] = w[t]
    w = [scr[f // planes, f % planes].T for f in range(nf)]
    for c, sends, takes in halos:
        pl.when(sends)(c.wait_send)
    for c in xm_copies + ym_copies + x_copies + y_copies:
        c.wait_send()

    for c in y_copies:
        c.wait_recv()
    low, high = ends_solve(yr_recv, il, ir, y_inner, dy, iy)
    blank = jnp.zeros((ny - 2 * SUB, nx), jnp.float32)
    ends = jnp.concatenate([low, high, blank], 0).T
    for f in range(nf):
        p = f % planes
        a = w[f] + y_left[p] * ends[:, f : f + 1] + y_right[p] * ends[:, SUB + f : SUB + f + 1]
        a = a.reshape(tx, SUB, ny)
        for t in range(tx):
            out[f // planes, p, pl.ds(t, SUB, stride=tx), :] = a[t]


def local(dx, dy, velocity, diffusion):
    ncomp, planes, nx, ny = velocity.shape
    vmem = pl.BlockSpec(memory_space=pltpu.VMEM)
    f32 = jnp.float32
    dma = pltpu.SemaphoreType.DMA
    return pl.pallas_call(
        functools.partial(kernel, dx, dy),
        out_shape=pltpu.VMEM(velocity.shape, f32),
        in_specs=[pl.BlockSpec(memory_space=pltpu.HBM)] * 2,
        out_specs=vmem,
        scratch_shapes=[
            pltpu.VMEM(velocity.shape, f32),
            pltpu.VMEM(diffusion.shape, f32),
            pltpu.VMEM((2, SUB, ny), f32),
            pltpu.VMEM((2, SUB, ny), f32),
            pltpu.VMEM((2 * SUB, nx), f32),
            pltpu.VMEM((2, 2 * SUB, nx), f32),
            pltpu.VMEM((dx, 2 * SUB, ny), f32),
            pltpu.VMEM((dy, 2 * SUB, nx), f32),
            pltpu.VMEM((dx, SUB, ny), f32),
            pltpu.VMEM((dx, SUB, ny), f32),
            pltpu.VMEM((dy, SUB, nx), f32),
            pltpu.VMEM((dy, SUB, nx), f32),
            pltpu.VMEM((ncomp, planes, ny, nx), f32),
            pltpu.VMEM((planes, ny, nx), f32),
            dma((2,)), dma((4,)), dma((4,)),
            dma((dx,)), dma((dx,)), dma((dx,)), dma((dx,)),
            dma((dy,)), dma((dy,)), dma((dy,)), dma((dy,)),
        ],
        compiler_params=pltpu.CompilerParams(
            collective_id=0, has_side_effects=True, vmem_limit_bytes=32 * 1024 * 1024
        ),
    )(
        pltpu.with_memory_space_constraint(velocity, pltpu.HBM),
        pltpu.with_memory_space_constraint(diffusion, pltpu.HBM),
    )


def solution(mesh):
    in_specs = (P(None, None, "gx", "gy"), P(None, "gx", "gy"))
    out_specs = P(None, None, "gx", "gy")
    body = functools.partial(local, mesh.shape["gx"], mesh.shape["gy"])
    return jax.shard_map(body, mesh=mesh, in_specs=in_specs, out_specs=out_specs, check_vma=False)
```

```python
import functools

import jax
import jax.numpy as jnp
from jax import lax
from jax.experimental import pallas as pl
from jax.experimental.pallas import tpu as pltpu
from jax.sharding import PartitionSpec as P

courant = 0.25
SUB = 8
MESH = pl.DeviceIdType.MESH


def halves(a):
    a = a.reshape((a.shape[0] // 2, 2) + a.shape[1:])
    return a[:, 0], a[:, 1]


def plus(a, b):
    return b if a is None else (a if b is None else a + b)


def join_matrix(c1, c2, gr1, gl2, gl1, gr2):
    g = gr1 + gl2
    r = 1.0 / (c1 + c2 + g)
    p, q = c1 * r, c2 * r
    return (p, q, r), p * c2, gl1 + p * g, gr2 + q * g


def tree_matrix(d, row):
    prev = jnp.concatenate([roll_rows(d[-1:], 1), d[:-1]], 0)
    c = 0.5 * (prev + d)
    kept = row == 0
    c1, c2 = halves(c)
    r = 1.0 / (c1 + c2 + 1.0)
    p, q = c1 * r, c2 * r
    p, q, r = (
        jnp.concatenate([jnp.where(kept, value, a[:1]), a[1:]], 0)
        for a, value in ((p, 1.0), (q, 0.0), (r, 0.0))
    )
    levels = [(p, q, r)]
    c, gl, gr = p * c2, p, 1.0 + q
    while c.shape[0] > 1:
        c1, c2 = halves(c)
        gr1, gr2 = halves(gr)
        gl1, gl2 = halves(gl)
        level, c, gl, gr = join_matrix(c1, c2, gr1, gl2, gl1, gr2)
        levels.append(level)
    return levels, c[0], gl[0], gr[0]


def tree_source(il, ir, levels, widen):
    mids = []
    for level in levels:
        p, q, r = (widen(a) for a in level)
        ir1, ir2 = halves(ir)
        il1, il2 = (None, None) if il is None else halves(il)
        i = plus(ir1, il2)
        mids.append(i * r)
        il = plus(il1, p * i)
        ir = ir2 + q * i
    return mids, il[0], ir[0]


def tree_down(left, right, levels, mids, widen):
    w = right[None]
    for level, mid in zip(reversed(levels), reversed(mids)):
        p, q = widen(level[0]), widen(level[1])
        wl = left[None] if w.shape[0] == 1 else jnp.concatenate([left[None], w[:-1]], 0)
        m = mid + p * wl + q * w
        w = jnp.stack([m, w], 1).reshape((2 * w.shape[0],) + w.shape[1:])
    return w


def roll_rows(a, shift):
    flat = a.reshape((-1,) + a.shape[-2:])
    out = [pltpu.roll(flat[k], shift % SUB, 0) for k in range(flat.shape[0])]
    return jnp.stack(out).reshape(a.shape)


def rows_matrix(c, gl, gr):
    levels = []
    for shift in (1, 2, 4):
        level, c, gl, gr = join_matrix(
            roll_rows(c, shift), c, roll_rows(gr, shift), gl, roll_rows(gl, shift), gr
        )
        levels.append(level)
    return levels, c, gl, gr


def rows_source(il, ir, levels):
    mids = []
    for shift, (p, q, r) in zip((1, 2, 4), levels):
        i = roll_rows(ir, shift) + il
        mids.append(i * r)
        il = roll_rows(il, shift) + p * i
        ir = ir + q * i
    return mids, il, ir


def rows_down(left, right, levels, mids, row):
    def solve(k, wl, wr):
        return mids[k] + levels[k][0] * wl + levels[k][1] * wr

    m = solve(2, left, right)
    m3 = jnp.broadcast_to(m[..., 7:8, :], m.shape)
    wr = jnp.where(row < 4, m3, right)
    m = solve(1, jnp.where(row < 4, left, m3), wr)
    m1 = jnp.broadcast_to(m[..., 3:4, :], m.shape)
    m5 = jnp.broadcast_to(m[..., 7:8, :], m.shape)
    wl = jnp.where(row < 2, left, jnp.where(row < 4, m1, jnp.where(row < 6, m3, m5)))
    wr = jnp.where(row < 2, m1, jnp.where(row < 4, m3, jnp.where(row < 6, m5, right)))
    m = solve(0, wl, wr)
    w = jnp.where(row % 2 == 1, wr, roll_rows(m, 7))
    return jnp.where(row == 0, left, roll_rows(w, 1)), w


def pick(place, items):
    out = items[0]
    for k in range(1, len(items)):
        out = jnp.where(place == k, items[k], out)
    return out


def tile_of(a, row):
    flat = a.reshape((-1,) + a.shape[-2:])
    out = jnp.zeros_like(flat[0])
    for f in range(flat.shape[0]):
        out = jnp.where(row == f, pltpu.roll(flat[f], (f + 1) % SUB, 0), out)
    return out


def put_matrix(ref, place, c, gl, gr, first, last):
    planes = c.shape[0]
    for p in range(planes):
        ref[place, p : p + 1, :] = c[p, SUB - 1 :]
        ref[place, planes + p : planes + p + 1, :] = gl[p, SUB - 1 :]
        ref[place, 2 * planes + p : 2 * planes + p + 1, :] = gr[p, SUB - 1 :]
        ref[place, 3 * planes + p : 3 * planes + p + 1, :] = first[p]
        ref[place, 4 * planes + p : 4 * planes + p + 1, :] = last[p]


def ends_matrix(ref, count, place, planes, row):
    def spread(k, quantity):
        return pick(
            row % planes,
            [ref[k, quantity * planes + p : quantity * planes + p + 1, :] for p in range(planes)],
        )

    c, gl, gr, first, last = ([spread(k, j) for k in range(count)] for j in range(5))
    link = [0.5 * (last[k - 1] + first[k]) if k else 0.5 * first[0] for k in range(count)]
    left, t_first, t_last = [gl[0] + link[0]], [], []
    right, u_first, u_last = [gr[-1] + 0.5 * last[-1]], [], []
    for k in range(count):
        t_first.append(c[k] / (c[k] + left[k]))
        g = gr[k] + t_first[k] * left[k]
        j = count - 1 - k
        u_last.insert(0, c[j] / (c[j] + right[0]))
        h = gl[j] + u_last[0] * right[0]
        if k < count - 1:
            t_last.append(link[k + 1] / (link[k + 1] + g))
            left.append(gl[k + 1] + t_last[k] * g)
            u_first.insert(0, link[j] / (link[j] + h))
            right.insert(0, gr[j - 1] + u_first[0] * h)
    u_first.insert(0, None)
    own_c, g, h = pick(place, c), pick(place, left), pick(place, right)
    r = 1.0 / (own_c * (g + h) + g * h)
    inner = ((own_c + h) * r, own_c * r, (own_c + g) * r)
    t_own, u_own = pick(place, t_first), pick(place, u_last)
    zero = jnp.zeros_like(own_c)
    from_first, from_last = [zero] * count, [zero] * count
    x = None
    for e in range(1, count):
        through = zero if x is None else x * t_first[e - 1] * t_last[e - 1]
        x = jnp.where(place == e - 1, t_last[e - 1], through)
        from_last[e], from_first[e] = x, x * t_own
    y = None
    for e in range(count - 2, -1, -1):
        through = zero if y is None else y * u_last[e + 1] * u_first[e + 1]
        y = jnp.where(place == e + 1, u_first[e + 1], through)
        from_first[e] = jnp.where(place > e, y, from_first[e])
        from_last[e] = jnp.where(place > e, y * u_own, from_last[e])
    return from_first, from_last, inner


def ends_send(send, il, ir, from_first, from_last, copies):
    for e in range(len(from_first)):
        send[e] = il * from_first[e] + ir * from_last[e]
    for c in copies:
        c.start()


def ends_solve(recv, il, ir, inner, count, place, ncomp, planes):
    for k in range(count):
        tile = recv[k]
        il = il + jnp.where(k < place, tile, 0.0)
        ir = ir + jnp.where(k > place, tile, 0.0)
    low = inner[0] * il + inner[1] * ir
    high = inner[1] * il + inner[2] * ir

    def split(a):
        parts = [jnp.broadcast_to(a[f : f + 1], a.shape) for f in range(ncomp * planes)]
        return jnp.stack(parts).reshape((ncomp, planes) + a.shape)

    return split(low), split(high)


def kernel(
    dx, dy, vel_in, dif_in, out,
    vel, dif, xh_send, xh_recv, yh_send, yh_recv,
    xm, ym, xr_send, xr_recv, yr_send, yr_recv, scr, scr_d,
    ins, hs, hr, xms, xmr, xs, xr, yms, ymr, ys, yr,
):
    ncomp, planes, nx, ny = vel.shape
    tx, ty = nx // SUB, ny // SUB
    nf = ncomp * planes
    ix, iy = lax.axis_index("gx"), lax.axis_index("gy")
    x_peers = [lax.rem(ix + o, dx) for o in range(1, dx)]
    y_peers = [lax.rem(iy + o, dy) for o in sorted(range(1, dy), key=lambda o: abs(2 * o - dy))]

    vel_copy = pltpu.make_async_copy(vel_in, vel, ins.at[0])
    dif_copy = pltpu.make_async_copy(dif_in, dif, ins.at[1])
    vel_copy.start()
    dif_copy.start()
    barrier = pltpu.get_barrier_semaphore()
    for peer in x_peers:
        pl.semaphore_signal(barrier, inc=1, device_id={"gx": peer}, device_id_type=MESH)
    for peer in y_peers:
        pl.semaphore_signal(barrier, inc=1, device_id={"gy": peer}, device_id_type=MESH)

    def copy(src, dst, send, recv, where):
        return pltpu.make_async_remote_copy(
            src_ref=src, dst_ref=dst, send_sem=send, recv_sem=recv,
            device_id=where, device_id_type=MESH,
        )

    def wide(a):
        return a[:, None]

    row = lax.broadcasted_iota(jnp.int32, (SUB, ny), 0)
    row_y = lax.broadcasted_iota(jnp.int32, (SUB, nx), 0)
    lane = lax.broadcasted_iota(jnp.int32, (nx, ny), 1)
    scale = 0.5 * courant

    vel_copy.wait()
    v = jnp.stack([vel[:, :, pl.ds(t, SUB, stride=tx), :] for t in range(tx)])
    fields = [v[:, c, p].reshape(nx, ny) for c in range(ncomp) for p in range(planes)]
    for f in range(nf):
        ref = vel.at[f // planes, f % planes]
        xh_send[0, f : f + 1, :] = ref[nx - 1 : nx, :]
        xh_send[1, f : f + 1, :] = ref[0:1, :]
    edges = jnp.zeros((nx, ny), jnp.float32)
    for f, a in enumerate(fields):
        edges = jnp.where(lane // 2 == f, pltpu.roll(a, 2 * f + 1, 1), edges)
    yh_send[...] = edges.T[: 2 * SUB]

    x_high, x_low = {"gx": lax.rem(ix + 1, dx)}, {"gx": lax.rem(ix + dx - 1, dx)}
    y_high, y_low = {"gy": lax.rem(iy + 1, dy)}, {"gy": lax.rem(iy + dy - 1, dy)}
    halos = [
        (copy(yh_send, yh_recv.at[0], hs.at[2], hr.at[2], y_high), iy < dy - 1, iy > 0),
        (copy(yh_send, yh_recv.at[1], hs.at[3], hr.at[3], y_low), iy > 0, iy < dy - 1),
        (copy(xh_send.at[0], xh_recv.at[0], hs.at[0], hr.at[0], x_high), ix < dx - 1, ix > 0),
        (copy(xh_send.at[1], xh_recv.at[1], hs.at[1], hr.at[1], x_low), ix > 0, ix < dx - 1),
    ]
    pl.semaphore_wait(barrier, dx + dy - 2)
    for c, sends, takes in halos:
        pl.when(sends)(c.start)

    dif_copy.wait()
    d = jnp.stack([dif[:, pl.ds(t, SUB, stride=tx), :] for t in range(tx)])
    xt, c, gl, gr = tree_matrix(d, row)
    xrow, c, gl, gr = rows_matrix(c, gl, gr)
    put_matrix(
        xm, ix, c, gl, gr, [dif[p, 0:1, :] for p in range(planes)],
        [dif[p, nx - 1 : nx, :] for p in range(planes)],
    )
    xm_copies = [
        copy(xm.at[ix], xm.at[ix], xms.at[o], xmr.at[o], {"gx": peer})
        for o, peer in enumerate(x_peers)
    ]
    for c in xm_copies:
        c.start()
    for p in range(planes):
        scr_d[p] = d[:, p].reshape(nx, ny).T
    dt = jnp.stack([scr_d[:, pl.ds(t, SUB, stride=ty), :] for t in range(ty)])
    yt, c, gl, gr = tree_matrix(dt, row_y)
    yrow, c, gl, gr = rows_matrix(c, gl, gr)
    put_matrix(
        ym, iy, c, gl, gr, [scr_d[p, 0:1, :] for p in range(planes)],
        [scr_d[p, ny - 1 : ny, :] for p in range(planes)],
    )
    ym_copies = [
        copy(ym.at[iy], ym.at[iy], yms.at[o], ymr.at[o], {"gy": peer})
        for o, peer in enumerate(y_peers)
    ]
    for c in ym_copies:
        c.start()

    source = []
    for cc in range(ncomp):
        for p in range(planes):
            f = cc * planes + p
            a = v[:, cc, p]
            lo = jnp.where(row == 0, 0.0, pltpu.roll(a[tx - 1], 1, 0))
            hi = jnp.where(row == SUB - 1, 0.0, pltpu.roll(a[0], SUB - 1, 0))
            grad_x = jnp.concatenate([a[1:], hi[None]], 0) - jnp.concatenate([lo[None], a[:-1]], 0)
            grad_y = jnp.where(lane == ny - 1, 0.0, pltpu.roll(fields[f], ny - 1, 1))
            grad_y = grad_y - jnp.where(lane == 0, 0.0, pltpu.roll(fields[f], 1, 1))
            grad_y = grad_y.reshape(tx, SUB, ny)
            source.append(a - scale * (v[:, 0, p] * grad_x + v[:, 1, p] * grad_y))
    side = jnp.where(lane == 0, scale, jnp.where(lane == ny - 1, -scale, 0.0))
    weight = [side * fields[planes + p] for p in range(planes)]

    for c in xm_copies:
        c.wait_recv()
    x_first, x_last, x_inner = ends_matrix(xm, dx, ix, planes, row)

    for c, sends, takes in halos:
        pl.when(takes)(c.wait_recv)
    take = lax.broadcasted_iota(jnp.int32, (2 * SUB, nx), 0) % 2 == 0
    halo = jnp.where(
        take,
        jnp.where(iy < dy - 1, pltpu.roll(yh_recv[1], 2 * SUB - 1, 0), 0.0),
        jnp.where(iy > 0, pltpu.roll(yh_recv[0], 1, 0), 0.0),
    )
    halo = jnp.where(lax.broadcasted_iota(jnp.int32, (2 * SUB, nx), 0) < 2 * nf, halo, 0.0)
    halo = jnp.concatenate([halo, jnp.zeros((ny - 2 * SUB, nx), jnp.float32)], 0).T
    for f in range(nf):
        near = pltpu.roll(halo, ny - 2 * f - 1, 1)
        source[f] = source[f] + (weight[f % planes] * near).reshape(tx, SUB, ny)
    source = jnp.stack(source, 1).reshape(v.shape)
    xmids, il, ir = tree_source(None, source, xt, wide)
    xrowmids, il, ir = rows_source(il, ir, xrow)
    own_first = pick(row % planes, [xh_send[1, p : p + 1, :] for p in range(planes)])
    own_last = pick(row % planes, [xh_send[0, p : p + 1, :] for p in range(planes)])
    il = tile_of(il, row) + scale * own_first * jnp.where(ix > 0, xh_recv[0], 0.0)
    ir = tile_of(ir, row) - scale * own_last * jnp.where(ix < dx - 1, xh_recv[1], 0.0)
    x_copies = [
        copy(xr_send.at[peer], xr_recv.at[ix], xs.at[o], xr.at[o], {"gx": peer})
        for o, peer in enumerate(x_peers)
    ]
    ends_send(xr_send, il, ir, x_first, x_last, x_copies)

    for c in ym_copies:
        c.wait_recv()
    y_first, y_last, y_inner = ends_matrix(ym, dy, iy, planes, row_y)

    for c in x_copies:
        c.wait_recv()
    low, high = ends_solve(xr_recv, il, ir, x_inner, dx, ix, ncomp, planes)
    left, right = rows_down(low, high, xrow, xrowmids, row)
    middle = tree_down(left, right, xt, xmids, wide)

    for f in range(nf):
        cc, p = f // planes, f % planes
        scr[cc, p] = middle[:, cc, p].reshape(nx, ny).T
    m = jnp.stack([scr[:, :, pl.ds(t, SUB, stride=ty), :] for t in range(ty)])
    ymids, il, ir = tree_source(None, m, yt, wide)
    yrowmids, il, ir = rows_source(il, ir, yrow)
    il, ir = tile_of(il, row_y), tile_of(ir, row_y)
    y_copies = [
        copy(yr_send.at[peer], yr_recv.at[iy], ys.at[o], yr.at[o], {"gy": peer})
        for o, peer in enumerate(y_peers)
    ]
    ends_send(yr_send, il, ir, y_first, y_last, y_copies)
    for c, sends, takes in halos:
        pl.when(sends)(c.wait_send)
    for c in xm_copies + ym_copies + x_copies + y_copies:
        c.wait_send()
    for c in y_copies:
        c.wait_recv()
    low, high = ends_solve(yr_recv, il, ir, y_inner, dy, iy, ncomp, planes)
    left, right = rows_down(low, high, yrow, yrowmids, row_y)
    w = tree_down(left, right, yt, ymids, wide)
    for t in range(ty):
        scr[:, :, pl.ds(t, SUB, stride=ty), :] = w[t]
    for f in range(nf):
        cc, p = f // planes, f % planes
        a = scr[cc, p].T.reshape(tx, SUB, ny)
        for t in range(tx):
            out[cc, p, pl.ds(t, SUB, stride=tx), :] = a[t]


def local(dx, dy, velocity, diffusion):
    ncomp, planes, nx, ny = velocity.shape
    vmem = pl.BlockSpec(memory_space=pltpu.VMEM)
    f32 = jnp.float32
    dma = pltpu.SemaphoreType.DMA
    return pl.pallas_call(
        functools.partial(kernel, dx, dy),
        out_shape=pltpu.VMEM(velocity.shape, f32),
        in_specs=[pl.BlockSpec(memory_space=pltpu.HBM)] * 2,
        out_specs=vmem,
        scratch_shapes=[
            pltpu.VMEM(velocity.shape, f32),
            pltpu.VMEM(diffusion.shape, f32),
            pltpu.VMEM((2, SUB, ny), f32),
            pltpu.VMEM((2, SUB, ny), f32),
            pltpu.VMEM((2 * SUB, nx), f32),
            pltpu.VMEM((2, 2 * SUB, nx), f32),
            pltpu.VMEM((dx, 2 * SUB, ny), f32),
            pltpu.VMEM((dy, 2 * SUB, nx), f32),
            pltpu.VMEM((dx, SUB, ny), f32),
            pltpu.VMEM((dx, SUB, ny), f32),
            pltpu.VMEM((dy, SUB, nx), f32),
            pltpu.VMEM((dy, SUB, nx), f32),
            pltpu.VMEM((ncomp, planes, ny, nx), f32),
            pltpu.VMEM((planes, ny, nx), f32),
            dma((2,)), dma((4,)), dma((4,)),
            dma((dx,)), dma((dx,)), dma((dx,)), dma((dx,)),
            dma((dy,)), dma((dy,)), dma((dy,)), dma((dy,)),
        ],
        compiler_params=pltpu.CompilerParams(
            collective_id=0, has_side_effects=True, vmem_limit_bytes=32 * 1024 * 1024
        ),
    )(
        pltpu.with_memory_space_constraint(velocity, pltpu.HBM),
        pltpu.with_memory_space_constraint(diffusion, pltpu.HBM),
    )


def solution(mesh):
    in_specs = (P(None, None, "gx", "gy"), P(None, "gx", "gy"))
    out_specs = P(None, None, "gx", "gy")
    body = functools.partial(local, mesh.shape["gx"], mesh.shape["gy"])
    return jax.shard_map(body, mesh=mesh, in_specs=in_specs, out_specs=out_specs, check_vma=False)
```
